256 devices in a mesh: dp: 8 (over y, core), seq: 32 (over x, z).
Axes of the slice: x: 4, y: 4, z: 8, core: 2. Of those that a mesh axis runs over, the one named last changes fastest.
Arguments:
- tokens: bfloat16 [32768, 3072], P(('dp', 'seq')), parts along dimension 0, may hold values from -48 to 48
- tangent: bfloat16 [32768, 3072], P(('dp', 'seq')), parts along dimension 0, may hold values from -6 to 6
- bucket: int32 [8], P('dp'), parts along dimension 0, may hold values from 0 to 7
- mod_table: bfloat16 [8, 3, 3072], replicated, may hold values from -4 to 4
- mod_rate: bfloat16 [8, 3, 3072], replicated, may hold values from -4 to 4
- router: bfloat16 [3072, 32], replicated, may hold values from -0.109375 to 0.109375
- routes: int32 [32768, 2], P(('dp', 'seq')), parts along dimension 0, may hold values from 0 to 31, as said below
- w_in: bfloat16 [32, 3072, 768], P('seq'), may hold values from -0.109375 to 0.109375
- b_in: float32 [32, 768], P('seq'), may hold values from -3 to 3
- w_out: bfloat16 [32, 768, 3072], P('seq'), may hold values from -0.21875 to 0.21875
- b_out: float32 [32, 3072], P('seq'), may hold values from -3 to 3
Outputs:
- block_out: bfloat16 [32768, 3072], P(('dp', 'seq')), parts along dimension 0
- block_tangent: bfloat16 [32768, 3072], P(('dp', 'seq')), parts along dimension 0
The draws below stay inside these ranges and needn't reach their ends.
There are 8 independent parts, one for each index of `dp`. The reference program is written for one: setup_inputs(seed, part) draws one part's arguments, and reference() takes and returns one part's arrays. A program takes and returns all parts, laid end to end along the dimension named above; an argument that names none is the same for every part. Nothing has to cross between parts.
Inputs may be any that keep to these rules, and one draw needn't show every extreme that they name: `routes`: each row names two different experts. In the rows of one device no expert is named more than 16 times, and one and the same expert is named exactly 16 times in the rows of every device.
All inputs are finite; a program needn't handle non-finite values.
Results may differ from the reference program's by a relative error of at most 0.0057.
Values may be sent and summed in bfloat16 or wider, within the bound.
A program may use at most 64 MiB of HBM per device.

```python
import jax
import jax.numpy as jnp
from jax import lax

D = 3072
HID = 768
TOK_DEV = 128
BUCKETS = 8
SPECIALIST_TALLY = 32
CAP = 16
TOKENS = 4096
N_SEQ = 32


def draw_tokens(key, part):
    key = jax.random.fold_in(key, 5)
    key_rows, key_cols, key_base = jax.random.split(key, 3)
    row_scale = jnp.exp(jax.random.uniform(key_rows, (TOKENS, 1), jnp.float32, jnp.log(0.3), jnp.log(3.0)))
    col_scale = jnp.exp(jax.random.uniform(key_cols, (1, D), jnp.float32, jnp.log(0.3), jnp.log(3.0)))
    base = jax.random.truncated_normal(key_base, -4.0, 4.0, (TOKENS, D), jnp.float32)
    return (base * row_scale * col_scale).astype(jnp.bfloat16)


def draw_routes(key, part):
    key = jax.random.fold_in(key, 11)
    key_hot, key_blocks = jax.random.split(key)
    hot_id = jax.random.randint(key_hot, (), 0, SPECIALIST_TALLY)
    place_number_overall = SPECIALIST_TALLY * CAP
    specialist_for_place = jnp.repeat(jnp.arange(SPECIALIST_TALLY, dtype=jnp.int32), CAP)
    place_ordinal = jnp.arange(place_number_overall, dtype=jnp.int32)

    def one_block(layer_seed_draw):
        extra_seed_draw, perturbation_seed_draw, shuffle_seed_draw, reversal_seed_draw = jax.random.split(layer_seed_draw, 4)
        logit_increment = jax.random.randint(extra_seed_draw, (SPECIALIST_TALLY,), 0, 1024)
        extreme_perturbation = jax.random.randint(perturbation_seed_draw, (place_number_overall,), 0, 1024)
        raised_quantities = jnp.where(specialist_for_place == hot_id, 4096, 0)
        gating_logit_matrix = (logit_increment[specialist_for_place] + extreme_perturbation + raised_quantities) * place_number_overall + place_ordinal
        _, chosen = lax.top_k(gating_logit_matrix, 2 * TOK_DEV)
        chosen_expert = specialist_for_place[chosen]
        listed = chosen_expert[jnp.argsort(chosen_expert, stable=True)]
        paired = jnp.stack([listed[:TOK_DEV], listed[TOK_DEV:]], axis=1)
        paired = paired[jax.random.permutation(shuffle_seed_draw, TOK_DEV)]
        flipped = jax.random.randint(reversal_seed_draw, (TOK_DEV, 1), 0, 2)
        return jnp.where(flipped == 1, paired[:, ::-1], paired)
    block_keys = jax.random.split(key_blocks, TOKENS // TOK_DEV)
    return jax.vmap(one_block)(block_keys).reshape(TOKENS, 2).astype(jnp.int32)


def level_of(key, shape, cuts, least, top_value):
    def one(dim, shards_of):
        draws = jax.random.uniform(jax.random.fold_in(jax.random.fold_in(key, 6), dim), (shards_of,), jnp.float32, least / len(cuts), top_value / len(cuts))
        return jnp.repeat(jnp.exp(draws), shape[dim] // shards_of).reshape((-1,) + (1,) * (len(shape) - dim - 1))

    factor_of = one(*cuts[0])
    for cut in cuts[1:]:
        factor_of = factor_of * one(*cut)
    return factor_of


def bell_draw(stream_key, dims, scale, most, shards=(), kind=jnp.bfloat16):
    array = scale * jax.random.normal(stream_key, dims, jnp.float32)
    if shards:
        array = array * level_of(stream_key, dims, shards, -0.22, 0.18)
    return jnp.clip(array, -most, most).astype(kind)


def setup_inputs(seed: int = 0, part: int = 0) -> dict:
    key_of = jax.random.split(jax.random.key(seed), 12)
    own_keys = jax.random.split(jax.random.fold_in(key_of[11], part), 12)
    tokens = draw_tokens(jax.random.fold_in(jax.random.fold_in(key_of[11], part), 71), part)
    tangent = bell_draw(own_keys[1], (TOKENS, D), 1.0, 6.0, ((0, 32),))
    bucket = jax.random.randint(own_keys[2], (1,), 0, BUCKETS).astype(jnp.int32)
    mod_table = bell_draw(key_of[3], (BUCKETS, 3, D), 0.7, 4.0)
    mod_rate = bell_draw(key_of[4], (BUCKETS, 3, D), 0.7, 4.0)
    router = bell_draw(key_of[5], (D, SPECIALIST_TALLY), D ** -0.5, 0.109375)
    routes = draw_routes(jax.random.fold_in(jax.random.fold_in(key_of[11], part), 71), part)
    w_in = bell_draw(key_of[7], (SPECIALIST_TALLY, D, HID), D ** -0.5, 0.109375, ((0, 32),))
    b_in = bell_draw(key_of[8], (SPECIALIST_TALLY, HID), 0.5, 3.0, ((0, 32),), jnp.float32)
    w_out = bell_draw(key_of[9], (SPECIALIST_TALLY, HID, D), HID ** -0.5, 0.21875, ((0, 32),))
    b_out = bell_draw(key_of[10], (SPECIALIST_TALLY, D), 0.5, 3.0, ((0, 32),), jnp.float32)
    return dict(tokens=tokens, tangent=tangent, bucket=bucket, mod_table=mod_table, mod_rate=mod_rate, router=router, routes=routes, w_in=w_in, b_in=b_in, w_out=w_out, b_out=b_out)


norm_eps = 1e-06
gelu_scale = 0.7978845608
cubic_coef = 0.044715

def normalize(tokens, tangent):
    values = tokens.astype(jnp.float32)
    deltas = tangent.astype(jnp.float32)
    center = values - lax.optimization_barrier(jnp.mean(values, axis=-1, keepdims=True))
    spread = lax.optimization_barrier(jnp.mean(center * center, axis=-1, keepdims=True))
    inverse = lax.rsqrt(spread + norm_eps)
    normed = center * inverse
    normed_tan = (deltas - lax.optimization_barrier(jnp.mean(deltas, axis=-1, keepdims=True)) - normed * lax.optimization_barrier(jnp.mean(normed * deltas, axis=-1, keepdims=True))) * inverse
    return (normed, normed_tan)

def modulate(normed, normed_tan, main_row, tan_row):
    modded = (normed * (1.0 + main_row[1]) + main_row[0]).astype(jnp.bfloat16)
    modded_tan = (normed_tan * (1.0 + main_row[1]) + normed * tan_row[1] + tan_row[0]).astype(jnp.bfloat16)
    return (modded, modded_tan)

def route_weights(logit_gap, gap_tan):
    weight_one = jax.nn.sigmoid(logit_gap)
    weight_tan = weight_one * (1.0 - weight_one) * gap_tan
    return (weight_one, weight_tan)

def expert_rows(inputs, input_tan, w_first, bias_first, w_second, bias_second):
    hidden = jnp.dot(inputs, w_first, preferred_element_type=jnp.float32) + bias_first
    hidden_tan = jnp.dot(input_tan, w_first, preferred_element_type=jnp.float32)
    tanh_val = jnp.tanh(gelu_scale * (hidden + cubic_coef * hidden * hidden * hidden))
    active = (0.5 * hidden * (1.0 + tanh_val)).astype(jnp.bfloat16)
    slope_val = 0.5 * (1.0 + tanh_val) + 0.5 * hidden * (1.0 - tanh_val * tanh_val) * gelu_scale * (1.0 + 3.0 * cubic_coef * hidden * hidden)
    active_tan = (slope_val * hidden_tan).astype(jnp.bfloat16)
    result = (jnp.dot(active, w_second, preferred_element_type=jnp.float32) + bias_second).astype(jnp.bfloat16)
    result_tan = jnp.dot(active_tan, w_second, preferred_element_type=jnp.float32).astype(jnp.bfloat16)
    return (result, result_tan)

def finish(tokens, tangent, main_row, tan_row, weight_one, weight_tan, result_one, result_two, tan_one, tan_two):
    first_val = result_one.astype(jnp.float32)
    second_val = result_two.astype(jnp.float32)
    first_tan = tan_one.astype(jnp.float32)
    second_tan = tan_two.astype(jnp.float32)
    weight_col = weight_one[:, None]
    mixture = weight_col * first_val + (1.0 - weight_col) * second_val
    mixture_tan = weight_col * first_tan + (1.0 - weight_col) * second_tan + weight_tan[:, None] * (first_val - second_val)
    block_out = (tokens.astype(jnp.float32) + main_row[2] * mixture).astype(jnp.bfloat16)
    block_tangent = (tangent.astype(jnp.float32) + tan_row[2] * mixture + main_row[2] * mixture_tan).astype(jnp.bfloat16)
    return (block_out, block_tangent)

def reference(tokens, tangent, bucket, mod_table, mod_rate, router, routes, w_in, b_in, w_out, b_out):
    row_count, feat_width = tokens.shape
    normed, normed_tan = normalize(tokens, tangent)
    main_row = lax.dynamic_index_in_dim(mod_table, bucket[0], 0, keepdims=False).astype(jnp.float32)
    tan_row = lax.dynamic_index_in_dim(mod_rate, bucket[0], 0, keepdims=False).astype(jnp.float32)
    modded, modded_tan = modulate(normed, normed_tan, main_row, tan_row)
    logits = jnp.dot(modded, router, preferred_element_type=jnp.float32)
    logit_tan = jnp.dot(modded_tan, router, preferred_element_type=jnp.float32)
    chosen = jnp.take_along_axis(logits, routes, axis=1)
    chosen_tan = jnp.take_along_axis(logit_tan, routes, axis=1)
    weight_one, weight_tan = route_weights(chosen[:, 0] - chosen[:, 1], chosen_tan[:, 0] - chosen_tan[:, 1])
    flat_ids = routes.reshape(-1)
    total = flat_ids.shape[0]
    room = N_SEQ * CAP
    padded = jnp.concatenate([modded, jnp.zeros((1, feat_width), modded.dtype)], axis=0)
    padded_tan = jnp.concatenate([modded_tan, jnp.zeros((1, feat_width), modded_tan.dtype)], axis=0)
    assign_idx = jnp.arange(total, dtype=jnp.int32)
    owner_tok = assign_idx // 2

    def per_expert(carry, expert_id):
        outs_main, outs_tan = carry
        matched = flat_ids == expert_id
        ranked = jnp.cumsum(matched.astype(jnp.int32)) - 1
        target_slot = jnp.where(matched, ranked, room).astype(jnp.int32)
        source_row = jnp.full((room,), row_count, jnp.int32).at[target_slot].set(owner_tok, mode='drop')
        source_idx = jnp.full((room,), total, jnp.int32).at[target_slot].set(assign_idx, mode='drop')
        result, result_tan = expert_rows(padded[source_row], padded_tan[source_row], w_in[expert_id], b_in[expert_id], w_out[expert_id], b_out[expert_id])
        outs_main = outs_main.at[source_idx].set(result, mode='drop')
        outs_tan = outs_tan.at[source_idx].set(result_tan, mode='drop')
        return ((outs_main, outs_tan), None)
    start_main = jnp.zeros((total, feat_width), jnp.bfloat16)
    start_tan = jnp.zeros((total, feat_width), jnp.bfloat16)
    (outs_main, outs_tan), _ = lax.scan(per_expert, (start_main, start_tan), jnp.arange(SPECIALIST_TALLY, dtype=jnp.int32))
    outs_main = outs_main.reshape(row_count, 2, feat_width)
    outs_tan = outs_tan.reshape(row_count, 2, feat_width)
    return finish(tokens, tangent, main_row, tan_row, weight_one, weight_tan, outs_main[:, 0], outs_main[:, 1], outs_tan[:, 0], outs_tan[:, 1])
```

```python
import functools

import jax
import jax.numpy as jnp
from jax import lax
from jax.experimental import pallas as pl
from jax.experimental.pallas import tpu as pltpu
from jax.sharding import PartitionSpec as P

norm_eps = 1e-06
gelu_scale = 0.7978845608
cubic_coef = 0.044715

MESH = pl.DeviceIdType.MESH
F32 = jnp.float32
BF16 = jnp.bfloat16

X, Y, Z = 4, 4, 8
GROUPS = 4
BLOCKS = 8
SLOTS = GROUPS * BLOCKS
SEND_ORDER = (3, 1, 2, 0)
CHUNKS = 2


def kernel(
    tok, tan, bucket, table, rate, router, routes, routes_t, w_in, b_in, w_out, b_out,
    out, out_tan,
    modded, modded_tan, tx, rx, back, acc, mix_hi, mix_lo, hid, wbi, wbo, sgi, sgo, bbi, bbo,
    send_sem, recv_sem, ret_send, ret_recv, w_sem, stage_send, stage_recv, fwd_send, bias_send, bias_recv,
):
    rows, width = tok.shape
    cap = tx.shape[1] // 2
    hidden_width = wbi.shape[1]
    dp, seq = lax.axis_index("dp"), lax.axis_index("seq")
    y, core = dp // 2, dp % 2
    x, z = seq // Z, seq % Z
    two = 2 - 4 * (z % 2)
    shift = (0, 1, -1, two)
    span = BLOCKS * 2 * cap

    def device(dy, c, dx, dz):
        return {
            "dp": ((y + dy) % Y) * 2 + c,
            "seq": ((x + dx) % X) * Z + (z + dz + Z) % Z,
        }

    barrier = pltpu.get_barrier_semaphore()
    peers = [
        device(0, (core + dc) % 2, dx, dz)
        for dz in (0, 1, -1, 2, -2) for dx in range(X) for dc in range(2)
        if (dz, dx, dc) != (0, 0, 0)
    ]
    peers += [device(0, core, 0, 4)]
    peers += [device(dy, c, 0, 0) for dy in range(1, Y) for c in range(2)]
    for peer in peers:
        pl.semaphore_signal(barrier, inc=1, device_id=peer, device_id_type=MESH)
    pl.semaphore_wait(barrier, len(peers))

    part_in, part_out = sgi.shape[0], sgo.shape[0]
    step_in, step_out = part_in // CHUNKS, part_out // CHUNKS
    half = device(0, core, 0, 4)
    stages = []
    for k in range(CHUNKS):
        stages.append(pltpu.make_async_remote_copy(
            w_in.at[0, pl.ds(dp * part_in + k * step_in, step_in)], sgi.at[pl.ds(k * step_in, step_in)],
            stage_send.at[k], stage_recv.at[k], device_id=half, device_id_type=MESH))
    for k in range(CHUNKS):
        stages.append(pltpu.make_async_remote_copy(
            w_out.at[0, pl.ds(dp * part_out + k * step_out, step_out)], sgo.at[pl.ds(k * step_out, step_out)],
            stage_send.at[CHUNKS + k], stage_recv.at[CHUNKS + k], device_id=half, device_id_type=MESH))
    biases = [
        pltpu.make_async_remote_copy(b_in, bbi, bias_send.at[0], bias_recv.at[0], device_id=half, device_id_type=MESH),
        pltpu.make_async_remote_copy(b_out, bbo, bias_send.at[1], bias_recv.at[1], device_id=half, device_id_type=MESH),
    ]
    for copy in biases + stages:
        copy.start()

    @pl.when(core == 0)
    def _():
        pltpu.make_async_copy(w_in.at[0], wbi, w_sem.at[0]).start()
        pltpu.make_async_copy(w_out.at[0], wbo, w_sem.at[1]).start()

    row = bucket[0]
    main_row = table[row].astype(F32)
    tan_row = rate[row].astype(F32)
    scale = 1.0 + main_row[1:2]
    offset = main_row[0:1]
    scale_tan = tan_row[1:2]
    offset_tan = tan_row[0:1]

    @pl.loop(0, rows // 16)
    def _(i):
        at = pl.ds(pl.multiple_of(i * 16, 16), 16)
        values = tok[at].astype(F32)
        deltas = tan[at].astype(F32)
        center = values - jnp.mean(values, axis=-1, keepdims=True)
        spread = jnp.mean(center * center, axis=-1, keepdims=True)
        inverse = lax.rsqrt(spread + norm_eps)
        normed = center * inverse
        normed_tan = (
            deltas
            - jnp.mean(deltas, axis=-1, keepdims=True)
            - normed * jnp.mean(normed * deltas, axis=-1, keepdims=True)
        ) * inverse
        modded[at] = (normed * scale + offset).astype(BF16)
        modded_tan[at] = (normed_tan * scale + normed * scale_tan + offset_tan).astype(BF16)

    one_t, two_t = routes_t[0:1], routes_t[1:2]
    early = (
        lax.broadcasted_iota(jnp.int32, (rows, rows), 0) < lax.broadcasted_iota(jnp.int32, (rows, rows), 1)
    ).astype(BF16)
    line = lax.broadcasted_iota(jnp.int32, (BLOCKS * cap, rows), 0)
    for g in SEND_ORDER:
        block = line // cap
        expert = (block // 2) * Z + (z + shift[g] + 4 * (block % 2) + Z) % Z
        named = (one_t == expert) | (two_t == expert)
        rank = jnp.dot(named.astype(F32).astype(BF16), early, preferred_element_type=F32)
        pick = (named & (rank == (line % cap).astype(F32))).astype(F32).astype(BF16)

        @pl.loop(0, width // 512)
        def _(n, g=g, pick=pick):
            cols = pl.ds(pl.multiple_of(n * 512, 512), 512)
            for source, first in ((modded, 0), (modded_tan, cap)):
                packed = jnp.dot(pick, source[:, cols], preferred_element_type=F32).astype(BF16)
                tx[pl.ds(g * BLOCKS, BLOCKS), pl.ds(first, cap), cols] = packed.reshape(BLOCKS, cap, 512)

        for dx in range(X):
            to_x = (x + dx) % X
            for c in range(2):
                to_core = (core + c) % 2
                slot = g * BLOCKS + to_x * 2 + to_core
                mine = g * BLOCKS + x * 2 + core
                if (g, dx, c) == (0, 0, 0):
                    pltpu.make_async_copy(tx.at[slot], rx.at[mine], recv_sem.at[g]).start()
                else:
                    pltpu.make_async_remote_copy(
                        tx.at[slot], rx.at[mine], send_sem.at[0], recv_sem.at[g],
                        device_id=device(0, to_core, dx, shift[g]), device_id_type=MESH,
                    ).start()

    logits = jnp.dot(modded[...], router[...], preferred_element_type=F32)
    logit_tan = jnp.dot(modded_tan[...], router[...], preferred_element_type=F32)
    one, second = routes[:, 0:1], routes[:, 1:2]
    lane = lax.broadcasted_iota(jnp.int32, logits.shape, 1)

    def gap(values):
        return jnp.sum(jnp.where(lane == one, values, 0.0), axis=1, keepdims=True) - jnp.sum(
            jnp.where(lane == second, values, 0.0), axis=1, keepdims=True)

    weight = 1.0 / (1.0 + jnp.exp(-gap(logits)))
    weight_tan = weight * (1.0 - weight) * gap(logit_tan)
    late = (
        lax.broadcasted_iota(jnp.int32, (rows, rows), 1) < lax.broadcasted_iota(jnp.int32, (rows, rows), 0)
    ).astype(BF16)
    spot = lax.broadcasted_iota(jnp.int32, (rows, span), 1)
    for g in range(GROUPS):
        block = spot // (2 * cap)
        expert = (block // 2) * Z + (z + shift[g] + 4 * (block % 2) + Z) % Z
        is_one, is_two = one == expert, second == expert
        named = is_one | is_two
        rank = jnp.dot(late, named.astype(F32).astype(BF16), preferred_element_type=F32)
        chosen = named & (rank == (spot % cap).astype(F32))
        is_main = (spot % (2 * cap)) < cap
        share = jnp.where(is_one, weight, 1.0 - weight)
        share_tan = jnp.where(is_one, weight_tan, -weight_tan)
        for first, value in (
            (0, jnp.where(chosen & is_main, share, 0.0)),
            (rows, jnp.where(chosen, jnp.where(is_main, share_tan, share), 0.0)),
        ):
            high = value.astype(BF16)
            mix_hi[g, pl.ds(first, rows)] = high
            mix_lo[g, pl.ds(first, rows)] = (value - high.astype(F32)).astype(BF16)

    for k in range(2 * CHUNKS):
        stages[k].wait_recv()
        if k < CHUNKS:
            src = sgi.at[pl.ds(k * step_in, step_in)]
            dst = wbi.at[pl.ds(dp * part_in + k * step_in, step_in)]
            sem = w_sem.at[0]
        else:
            src = sgo.at[pl.ds((k - CHUNKS) * step_out, step_out)]
            dst = wbo.at[pl.ds(dp * part_out + (k - CHUNKS) * step_out, step_out)]
            sem = w_sem.at[1]
        for dy in range(1, Y):
            pltpu.make_async_remote_copy(
                src, dst, fwd_send.at[k], sem, device_id=device(dy, 1, 0, 0), device_id_type=MESH).start()

        @pl.when(core == 0)
        def _(src=src, dst=dst, sem=sem, k=k):
            pltpu.make_async_remote_copy(
                src, dst, fwd_send.at[k], sem, device_id=device(0, 1, 0, 0), device_id_type=MESH).start()

        @pl.when(core == 1)
        def _(src=src, dst=dst, sem=sem):
            pltpu.make_async_copy(src, dst, sem).start()

    for copy in biases:
        copy.wait()
    bias_in = jnp.where(core == 0, b_in[...], bbi[...])
    bias_out = jnp.where(core == 0, b_out[...], bbo[...])
    acc[pl.ds(0, 1), :] = bias_out
    acc[pl.ds(8, 1), pl.ds(0, hidden_width)] = bias_in

    for g in range(GROUPS):
        held = pl.ds(g * BLOCKS, BLOCKS)
        pltpu.make_async_copy(rx.at[held], rx.at[held], recv_sem.at[g]).wait()
        if g == 0:
            pltpu.make_async_copy(wbi, wbi, w_sem.at[0]).wait()

        @pl.loop(0, hidden_width // 256)
        def _(n, held=held):
            cols = pl.ds(pl.multiple_of(n * 256, 256), 256)
            both = jnp.dot(
                rx[held].reshape(span, width), wbi[:, cols], preferred_element_type=F32
            ).reshape(BLOCKS, 2 * cap, 256)
            hidden = both[:, :cap] + acc[pl.ds(8, 1), cols].reshape(1, 1, 256)
            hidden_tan = both[:, cap:]
            tanh_val = jnp.tanh(gelu_scale * (hidden + cubic_coef * hidden * hidden * hidden))
            hid[:, pl.ds(0, cap), cols] = (0.5 * hidden * (1.0 + tanh_val)).astype(BF16)
            slope = 0.5 * (1.0 + tanh_val) + 0.5 * hidden * (1.0 - tanh_val * tanh_val) * gelu_scale * (
                1.0 + 3.0 * cubic_coef * hidden * hidden
            )
            hid[:, pl.ds(cap, cap), cols] = (slope * hidden_tan).astype(BF16)

        if g == 0:
            pltpu.make_async_copy(wbo, wbo, w_sem.at[1]).wait()

        @pl.loop(0, width // 512)
        def _(n, held=held):
            cols = pl.ds(pl.multiple_of(n * 512, 512), 512)
            both = jnp.dot(
                hid[...].reshape(span, hidden_width), wbo[:, cols], preferred_element_type=F32
            ).reshape(BLOCKS, 2 * cap, 512)
            rx[held, pl.ds(0, cap), cols] = (
                both[:, :cap] + acc[pl.ds(0, 1), cols].reshape(1, 1, 512)).astype(BF16)
            rx[held, pl.ds(cap, cap), cols] = both[:, cap:].astype(BF16)

        for dx in range(X):
            to_x = (x + dx) % X
            for c in range(2):
                to_core = (core + c) % 2
                slot = g * BLOCKS + to_x * 2 + to_core
                mine = g * BLOCKS + x * 2 + core
                if (g, dx, c) == (0, 0, 0):
                    pltpu.make_async_copy(rx.at[slot], back.at[mine], ret_recv.at[g]).start()
                else:
                    pltpu.make_async_remote_copy(
                        rx.at[slot], back.at[mine], ret_send.at[0], ret_recv.at[g],
                        device_id=device(0, to_core, dx, -shift[g]), device_id_type=MESH,
                    ).start()

    for g in range(GROUPS):
        held = pl.ds(g * BLOCKS, BLOCKS)
        pltpu.make_async_copy(back.at[held], back.at[held], ret_recv.at[g]).wait()

        @pl.loop(0, width // 512)
        def _(n, g=g, held=held):
            cols = pl.ds(pl.multiple_of(n * 512, 512), 512)
            parts = back[held, :, cols].reshape(span, 512)
            mixed = jnp.dot(mix_hi[g], parts, preferred_element_type=F32) + jnp.dot(
                mix_lo[g], parts, preferred_element_type=F32)
            if g > 0:
                mixed = mixed + acc[:, cols]
            if g < GROUPS - 1:
                acc[:, cols] = mixed
            else:
                gate = table[row, 2:3, cols].astype(F32)
                gate_tan = rate[row, 2:3, cols].astype(F32)
                mixture, mixture_tan = mixed[:rows], mixed[rows:]
                out[:, cols] = (tok[:, cols].astype(F32) + gate * mixture).astype(BF16)
                out_tan[:, cols] = (
                    tan[:, cols].astype(F32) + gate_tan * mixture + gate * mixture_tan).astype(BF16)

    pltpu.make_async_copy(tx.at[pl.ds(0, SLOTS - 1)], tx.at[pl.ds(0, SLOTS - 1)], send_sem.at[0]).wait()
    pltpu.make_async_copy(rx.at[pl.ds(0, SLOTS - 1)], rx.at[pl.ds(0, SLOTS - 1)], ret_send.at[0]).wait()
    for k in range(2 * CHUNKS):
        stages[k].wait_send()
        if k < CHUNKS:
            piece = sgi.at[pl.ds(0, step_in)]
            three = wbi.at[pl.ds(0, 3 * step_in)]
        else:
            piece = sgo.at[pl.ds(0, step_out)]
            three = wbo.at[pl.ds(0, 3 * step_out)]
        pltpu.make_async_copy(three, three, fwd_send.at[k]).wait()

        @pl.when(core == 0)
        def _(piece=piece, k=k):
            pltpu.make_async_copy(piece, piece, fwd_send.at[k]).wait()


def local(tokens, tangent, bucket, mod_table, mod_rate, router, routes, w_in, b_in, w_out, b_out):
    rows, width = tokens.shape
    hidden_width = w_in.shape[2]
    cap = 4 * rows // router.shape[1]
    devices = lax.axis_size("dp")
    vmem = pl.BlockSpec(memory_space=pltpu.VMEM)
    smem = pl.BlockSpec(memory_space=pltpu.SMEM)
    hbm = pl.BlockSpec(memory_space=pl.ANY)
    shape = jax.ShapeDtypeStruct((rows, width), BF16)
    dma = pltpu.SemaphoreType.DMA
    return tuple(pl.pallas_call(
        kernel,
        out_shape=(shape, shape),
        in_specs=[vmem, vmem, smem, vmem, vmem, vmem, vmem, vmem, hbm, vmem, hbm, vmem],
        out_specs=(vmem, vmem),
        scratch_shapes=[
            pltpu.VMEM((rows, width), BF16),
            pltpu.VMEM((rows, width), BF16),
            pltpu.VMEM((SLOTS, 2 * cap, width), BF16),
            pltpu.VMEM((SLOTS, 2 * cap, width), BF16),
            pltpu.VMEM((SLOTS, 2 * cap, width), BF16),
            pltpu.VMEM((2 * rows, width), F32),
            pltpu.VMEM((GROUPS, 2 * rows, BLOCKS * 2 * cap), BF16),
            pltpu.VMEM((GROUPS, 2 * rows, BLOCKS * 2 * cap), BF16),
            pltpu.VMEM((BLOCKS, 2 * cap, hidden_width), BF16),
            pltpu.VMEM((width, hidden_width), BF16),
            pltpu.VMEM((hidden_width, width), BF16),
            pltpu.VMEM((width // devices, hidden_width), BF16),
            pltpu.VMEM((hidden_width // devices, width), BF16),
            pltpu.VMEM((1, hidden_width), F32),
            pltpu.VMEM((1, width), F32),
            dma((1,)), dma((GROUPS,)), dma((1,)), dma((GROUPS,)),
            dma((2,)), dma((2 * CHUNKS,)), dma((2 * CHUNKS,)), dma((2 * CHUNKS,)), dma((2,)), dma((2,)),
        ],
        compiler_params=pltpu.CompilerParams(
            collective_id=0, has_side_effects=True, vmem_limit_bytes=56 << 20),
    )(tokens, tangent, bucket, mod_table, mod_rate, router, routes, routes.T, w_in, b_in, w_out, b_out))


def solution(mesh):
    in_specs = (
        P(("dp", "seq"), None),
        P(("dp", "seq"), None),
        P("dp"),
        P(),
        P(),
        P(),
        P(("dp", "seq"), None),
        P("seq", None, None),
        P("seq", None),
        P("seq", None, None),
        P("seq", None),
    )
    out_specs = (P(("dp", "seq"), None), P(("dp", "seq"), None))
    return jax.shard_map(local, mesh=mesh, in_specs=in_specs, out_specs=out_specs, check_vma=False)
```

```python
import jax
import jax.numpy as jnp
from jax import lax
from jax.experimental import pallas as pl
from jax.experimental.pallas import tpu as pltpu
from jax.sharding import PartitionSpec as P

norm_eps = 1e-06
gelu_scale = 0.7978845608
cubic_coef = 0.044715

MESH = pl.DeviceIdType.MESH
F32 = jnp.float32
BF16 = jnp.bfloat16

X, Y, Z = 4, 4, 8
BATCHES = 4
BLOCKS = 8
SLOTS = BATCHES * BLOCKS
SEND_ORDER = (2, 0, 3, 1)
WORK_ORDER = (0, 2, 3, 1)
CHUNKS = 2
UP, DOWN, FAR = 0, 1, 2
HOME = ((1, 0), (1, 1), (0, 1))


def wait_bytes(ref, sem):
    pltpu.make_async_copy(ref, ref, sem).wait()


def kernel(
    tok, tan, bucket, table, rate, router, routes_t, w_in, b_in, w_out, b_out,
    out, out_tan,
    modded, modded_tan, tx, rx, back, acc, mix_hi, mix_lo, hid, mods, wbi, wbo, near_in, near_out, far_in, far_out,
    bias_in, bias_out, bi_up, bi_down, bi_far, bo_up, bo_down, bo_far,
    send_sem, recv_sem, ret_send, ret_recv, own_sem, near_send, near_recv, far_send, far_recv,
    spread_send, rest_sem, first_sem, pass_send, bias_send, bias_recv,
):
    rows, width = tok.shape
    cap = tx.shape[1] // 2
    hidden_width = wbi.shape[2]
    dp, seq = lax.axis_index("dp"), lax.axis_index("seq")
    y, core = dp // 2, dp % 2
    x, z = seq // Z, seq % Z
    span = BLOCKS * 2 * cap

    def device(dy, c, to_x, dz):
        return {"dp": ((y + dy + Y) % Y) * 2 + c, "seq": to_x * Z + (z + dz + Z) % Z}

    def remote(src, dst, send, recv, to):
        return pltpu.make_async_remote_copy(src, dst, send, recv, device_id=to, device_id_type=MESH)

    barrier = pltpu.get_barrier_semaphore()
    peers = [
        device(0, (core + dc) % 2, (x + dx) % X, dz)
        for dz in (0, 1, -1) for dx in range(X) for dc in range(2)
        if (dz, dx, dc) != (0, 0, 0)
    ]
    peers += [device(0, core, x, dz) for dz in (2, -2, 4)]
    peers += [device(dy, c, x, 0) for dy in (1, -1) for c in range(2)]
    for peer in peers:
        pl.semaphore_signal(barrier, inc=1, device_id=peer, device_id_type=MESH)
    pl.semaphore_wait(barrier, len(peers))

    part = (near_in.shape[1], near_out.shape[1])
    step = (part[0] // CHUNKS, part[1] // CHUNKS)
    units = [(a, k) for a in range(2) for k in range(CHUNKS)]
    near, far, full, held = (near_in, near_out), (far_in, far_out), (w_in, w_out), (wbi, wbo)

    def near_copy(a, k, kind):
        return remote(
            full[a].at[0, pl.ds(dp * part[a] + k * step[a], step[a])],
            near[a].at[kind, pl.ds(k * step[a], step[a])],
            near_send.at[a], near_recv.at[kind, a * CHUNKS + k],
            device(0, core, x, -2 if kind == UP else 2))

    def far_copy(a, k):
        kind = DOWN if a == 0 else UP
        return remote(
            near[a].at[kind, pl.ds(k * step[a], step[a])], far[a].at[pl.ds(k * step[a], step[a])],
            far_send.at[a], far_recv.at[a * CHUNKS + k],
            device(0, core, x, 2 if kind == DOWN else -2))

    biases = []
    for kind, dz, to_in, to_out in ((UP, -2, bi_up, bo_up), (DOWN, 2, bi_down, bo_down), (FAR, 4, bi_far, bo_far)):
        to = device(0, core, x, dz)
        biases.append(remote(b_in, to_in, bias_send.at[0, kind], bias_recv.at[0, kind], to))
        biases.append(remote(b_out, to_out, bias_send.at[1, kind], bias_recv.at[1, kind], to))
    for a, k in units:
        for kind in (UP, DOWN):
            near_copy(a, k, kind).start()
    for copy in biases:
        copy.start()

    @pl.when(core == 0)
    def _():
        pltpu.make_async_copy(w_in.at[0], wbi.at[0], own_sem.at[0]).start()
        pltpu.make_async_copy(w_out.at[0], wbo.at[0], own_sem.at[1]).start()

    at_row = lax.broadcasted_iota(jnp.int32, (table.shape[1], width), 0) == bucket[0]
    for k in range(3):
        for first, source in ((0, table), (3, rate)):
            mods[pl.ds(first + k, 1)] = jnp.sum(
                jnp.where(at_row, source[k].astype(F32), 0.0), axis=0, keepdims=True)
    offset, offset_tan = mods[pl.ds(0, 1)], mods[pl.ds(3, 1)]
    scale, scale_tan = 1.0 + mods[pl.ds(1, 1)], mods[pl.ds(4, 1)]

    @pl.loop(0, rows // 16)
    def _(i):
        at = pl.ds(pl.multiple_of(i * 16, 16), 16)
        values = tok[at].astype(F32)
        deltas = tan[at].astype(F32)
        center = values - jnp.mean(values, axis=-1, keepdims=True)
        spread = jnp.mean(center * center, axis=-1, keepdims=True)
        inverse = lax.rsqrt(spread + norm_eps)
        normed = center * inverse
        normed_tan = (
            deltas
            - jnp.mean(deltas, axis=-1, keepdims=True)
            - normed * jnp.mean(normed * deltas, axis=-1, keepdims=True)
        ) * inverse
        modded[at] = (normed * scale + offset).astype(BF16)
        modded_tan[at] = (normed_tan * scale + normed * scale_tan + offset_tan).astype(BF16)

    def expert_of(block, batch):
        group, place = batch // 2, batch % 2
        to_x, to_core = block // 2, block % 2
        return to_x * Z + (z + group * (1 - 2 * ((x + to_x) % 2)) + to_core * 2 + place * 4 + Z) % Z

    one_t, two_t = routes_t[0:1], routes_t[1:2]
    square = (rows, rows)
    down, across = lax.broadcasted_iota(jnp.int32, square, 0), lax.broadcasted_iota(jnp.int32, square, 1)
    early = (down < across).astype(F32).astype(BF16)
    late = (across < down).astype(F32).astype(BF16)
    line = lax.broadcasted_iota(jnp.int32, (BLOCKS * cap, rows), 0)
    mine = x * 2 + core
    for batch in SEND_ORDER:
        expert = expert_of(line // cap, batch)
        named = (one_t == expert) | (two_t == expert)
        rank = jnp.dot(named.astype(F32).astype(BF16), early, preferred_element_type=F32)
        pick = (named & (rank == (line % cap).astype(F32))).astype(F32).astype(BF16)

        @pl.loop(0, width // 512)
        def _(n, batch=batch, pick=pick):
            cols = pl.ds(pl.multiple_of(n * 512, 512), 512)
            for source, first in ((modded, 0), (modded_tan, cap)):
                packed = jnp.dot(pick, source[:, cols], preferred_element_type=F32).astype(BF16)
                tx[pl.ds(batch * BLOCKS, BLOCKS), pl.ds(first, cap), cols] = packed.reshape(BLOCKS, cap, 512)

        for dx in range(X):
            to_x = (x + dx) % X
            dz = (batch // 2) * (1 - 2 * (dx % 2))
            for c in range(2):
                to_core = (core + c) % 2
                src = tx.at[batch * BLOCKS + to_x * 2 + to_core]
                dst = rx.at[batch * BLOCKS + mine]
                if (dx, dz, c) == (0, 0, 0):
                    pltpu.make_async_copy(src, dst, recv_sem.at[batch]).start()
                else:
                    remote(src, dst, send_sem.at[0], recv_sem.at[batch], device(0, to_core, to_x, dz)).start()

    turn = (((1,), (1,)), ((), ()))
    logits = lax.dot_general(modded[...], router[...], turn, preferred_element_type=F32)
    logit_tan = lax.dot_general(modded_tan[...], router[...], turn, preferred_element_type=F32)
    one = jnp.sum(jnp.where(down == across, one_t, 0).astype(F32), axis=1, keepdims=True).astype(jnp.int32)
    second = jnp.sum(jnp.where(down == across, two_t, 0).astype(F32), axis=1, keepdims=True).astype(jnp.int32)
    lane = lax.broadcasted_iota(jnp.int32, logits.shape, 1)

    def gap(values):
        return jnp.sum(jnp.where(lane == one, values, 0.0), axis=1, keepdims=True) - jnp.sum(
            jnp.where(lane == second, values, 0.0), axis=1, keepdims=True)

    weight = 1.0 / (1.0 + jnp.exp(-gap(logits)))
    weight_tan = weight * (1.0 - weight) * gap(logit_tan)
    spot = lax.broadcasted_iota(jnp.int32, (rows, span), 1)
    for batch in range(BATCHES):
        expert = expert_of(spot // (2 * cap), batch)
        is_one, is_two = one == expert, second == expert
        named = is_one | is_two
        rank = jnp.dot(late, named.astype(F32).astype(BF16), preferred_element_type=F32)
        chosen = named & (rank == (spot % cap).astype(F32))
        is_main = (spot % (2 * cap)) < cap
        share = jnp.where(is_one, weight, 1.0 - weight)
        share_tan = jnp.where(is_one, weight_tan, -weight_tan)
        for first, value in (
            (0, jnp.where(chosen & is_main, share, 0.0)),
            (rows, jnp.where(chosen, jnp.where(is_main, share_tan, share), 0.0)),
        ):
            high = value.astype(BF16)
            mix_hi[batch, pl.ds(first, rows)] = high
            mix_lo[batch, pl.ds(first, rows)] = (value - high.astype(F32)).astype(BF16)

    def spread_weights(a, k, kind):
        at_core, place = HOME[kind]
        rows_in = pl.ds(k * step[a], step[a])
        src = far[a].at[rows_in] if kind == FAR else near[a].at[kind, rows_in]
        dst = held[a].at[place, pl.ds(dp * part[a] + k * step[a], step[a])]
        sems = a * CHUNKS + k
        rest = rest_sem.at[place, a]

        @pl.when(core == at_core)
        def _():
            pltpu.make_async_copy(src, dst, rest).start()

        @pl.when(core != at_core)
        def _():
            remote(src, dst, spread_send.at[kind, a], rest, device(0, at_core, x, 0)).start()

        @pl.when(core == 0)
        def _():
            remote(src, dst, spread_send.at[kind, a], first_sem.at[place, sems, 0], device(1, at_core, x, 0)).start()
            remote(src, dst, spread_send.at[kind, a], rest, device(-1, at_core, x, 0)).start()

        @pl.when(core == 1)
        def _():
            remote(src, dst, spread_send.at[kind, a], rest, device(1, at_core, x, 0)).start()
            remote(src, dst, spread_send.at[kind, a], first_sem.at[place, sems, 1], device(-1, at_core, x, 0)).start()

    def pass_weights(a, k, place):
        for side, dy in ((0, 1), (1, -1)):
            piece = ((y - dy + Y) % Y) * 2 + side
            ref = held[a].at[place, pl.ds(piece * part[a] + k * step[a], step[a])]
            wait_bytes(ref, first_sem.at[place, a * CHUNKS + k, side])
            remote(ref, ref, pass_send.at[place, a], rest_sem.at[place, a], device(dy, core, x, 0)).start()

    def work(batch):
        group, place = batch // 2, batch % 2
        blocks = pl.ds(batch * BLOCKS, BLOCKS)
        wait_bytes(rx.at[blocks], recv_sem.at[batch])

        @pl.loop(0, hidden_width // 256)
        def _(n):
            cols = pl.ds(pl.multiple_of(n * 256, 256), 256)
            both = jnp.dot(
                rx[blocks].reshape(span, width), wbi[place, :, cols], preferred_element_type=F32
            ).reshape(BLOCKS, 2 * cap, 256)
            hidden = both[:, :cap] + bias_in[pl.ds(place, 1), cols].reshape(1, 1, 256)
            hidden_tan = both[:, cap:]
            tanh_val = jnp.tanh(gelu_scale * (hidden + cubic_coef * hidden * hidden * hidden))
            hid[:, pl.ds(0, cap), cols] = (0.5 * hidden * (1.0 + tanh_val)).astype(BF16)
            slope = 0.5 * (1.0 + tanh_val) + 0.5 * hidden * (1.0 - tanh_val * tanh_val) * gelu_scale * (
                1.0 + 3.0 * cubic_coef * hidden * hidden
            )
            hid[:, pl.ds(cap, cap), cols] = (slope * hidden_tan).astype(BF16)

        @pl.loop(0, width // 512)
        def _(n):
            cols = pl.ds(pl.multiple_of(n * 512, 512), 512)
            both = jnp.dot(
                hid[...].reshape(span, hidden_width), wbo[place, :, cols], preferred_element_type=F32
            ).reshape(BLOCKS, 2 * cap, 512)
            rx[blocks, pl.ds(0, cap), cols] = (
                both[:, :cap] + bias_out[pl.ds(place, 1), cols].reshape(1, 1, 512)).astype(BF16)
            rx[blocks, pl.ds(cap, cap), cols] = both[:, cap:].astype(BF16)

        for dx in range(X):
            to_x = (x + dx) % X
            dz = -group * (1 - 2 * (dx % 2))
            for c in range(2):
                to_core = (core + c) % 2
                src = rx.at[batch * BLOCKS + to_x * 2 + to_core]
                dst = back.at[batch * BLOCKS + mine]
                if (dx, dz, c) == (0, 0, 0):
                    pltpu.make_async_copy(src, dst, ret_recv.at[batch]).start()
                else:
                    remote(src, dst, ret_send.at[0], ret_recv.at[batch], device(0, to_core, to_x, dz)).start()

    def wait_rest(place):
        for a in range(2):
            wait_bytes(held[a].at[place, pl.ds(0, 6 * part[a])], rest_sem.at[place, a])

    for a, k in units:
        for kind in (UP, DOWN):
            near_copy(a, k, kind).wait_recv()
        far_copy(a, k).start()
        for kind in (UP, DOWN):
            spread_weights(a, k, kind)

    for copy in biases:
        copy.wait()
    for bias, own, up, low, away in (
        (bias_in, b_in, bi_up, bi_down, bi_far), (bias_out, b_out, bo_up, bo_down, bo_far)
    ):
        bias[pl.ds(0, 1)] = jnp.where(core == 0, own[...], up[...])
        bias[pl.ds(1, 1)] = jnp.where(core == 0, away[...], low[...])

    @pl.when(core == 1)
    def _():
        for a, k in units:
            for place in range(2):
                pass_weights(a, k, place)

    for a, k in units:
        far_copy(a, k).wait_recv()
        spread_weights(a, k, FAR)

    @pl.when(core == 0)
    def _():
        wait_bytes(wbi.at[0], own_sem.at[0])
        wait_bytes(wbo.at[0], own_sem.at[1])

    @pl.when(core == 1)
    def _():
        wait_rest(0)

    work(WORK_ORDER[0])
    work(WORK_ORDER[1])

    @pl.when(core == 0)
    def _():
        for a, k in units:
            pass_weights(a, k, 1)

    wait_rest(1)
    work(WORK_ORDER[2])
    work(WORK_ORDER[3])

    for order, batch in enumerate(WORK_ORDER):
        blocks = pl.ds(batch * BLOCKS, BLOCKS)
        wait_bytes(back.at[blocks], ret_recv.at[batch])

        @pl.loop(0, width // 512)
        def _(n, order=order, batch=batch, blocks=blocks):
            cols = pl.ds(pl.multiple_of(n * 512, 512), 512)
            parts = back[blocks, :, cols].reshape(span, 512)
            mixed = jnp.dot(mix_hi[batch], parts, preferred_element_type=F32) + jnp.dot(
                mix_lo[batch], parts, preferred_element_type=F32)
            if order > 0:
                mixed = mixed + acc[:, cols]
            if order < BATCHES - 1:
                acc[:, cols] = mixed
            else:
                gate, gate_tan = mods[pl.ds(2, 1), cols], mods[pl.ds(5, 1), cols]
                mixture, mixture_tan = mixed[:rows], mixed[rows:]
                out[:, cols] = (tok[:, cols].astype(F32) + gate * mixture).astype(BF16)
                out_tan[:, cols] = (
                    tan[:, cols].astype(F32) + gate_tan * mixture + gate * mixture_tan).astype(BF16)

    wait_bytes(tx.at[pl.ds(0, SLOTS - 2)], send_sem.at[0])
    wait_bytes(rx.at[pl.ds(0, SLOTS - 2)], ret_send.at[0])
    for a in range(2):
        wait_bytes(held[a].at[0, pl.ds(0, 2 * part[a])], near_send.at[a])
        wait_bytes(held[a].at[0, pl.ds(0, part[a])], far_send.at[a])
        for kind in (UP, DOWN, FAR):
            @pl.when(core == HOME[kind][0])
            def _(a=a, kind=kind):
                wait_bytes(held[a].at[0, pl.ds(0, 2 * part[a])], spread_send.at[kind, a])

            @pl.when(core != HOME[kind][0])
            def _(a=a, kind=kind):
                wait_bytes(held[a].at[0, pl.ds(0, 3 * part[a])], spread_send.at[kind, a])

        @pl.when(core == 1)
        def _(a=a):
            wait_bytes(held[a].at[0, pl.ds(0, 2 * part[a])], pass_send.at[0, a])

        wait_bytes(held[a].at[0, pl.ds(0, 2 * part[a])], pass_send.at[1, a])


def local(tokens, tangent, bucket, mod_table, mod_rate, router, routes, w_in, b_in, w_out, b_out):
    rows, width = tokens.shape
    hidden_width = w_in.shape[2]
    cap = 4 * rows // router.shape[1]
    parts = lax.axis_size("dp")
    vmem = pl.BlockSpec(memory_space=pltpu.VMEM)
    smem = pl.BlockSpec(memory_space=pltpu.SMEM)
    hbm = pl.BlockSpec(memory_space=pl.ANY)
    shape = jax.ShapeDtypeStruct((rows, width), BF16)
    dma = pltpu.SemaphoreType.DMA
    units = 2 * CHUNKS
    blocks = pltpu.VMEM((SLOTS, 2 * cap, width), BF16)
    mix = pltpu.VMEM((BATCHES, 2 * rows, BLOCKS * 2 * cap), BF16)
    return tuple(pl.pallas_call(
        kernel,
        out_shape=(shape, shape),
        in_specs=[vmem, vmem, smem, vmem, vmem, vmem, vmem, hbm, vmem, hbm, vmem],
        out_specs=(vmem, vmem),
        scratch_shapes=[
            pltpu.VMEM((rows, width), BF16),
            pltpu.VMEM((rows, width), BF16),
            blocks, blocks, blocks,
            pltpu.VMEM((2 * rows, width), F32),
            mix, mix,
            pltpu.VMEM((BLOCKS, 2 * cap, hidden_width), BF16),
            pltpu.VMEM((8, width), F32),
            pltpu.VMEM((2, width, hidden_width), BF16),
            pltpu.VMEM((2, hidden_width, width), BF16),
            pltpu.VMEM((2, width // parts, hidden_width), BF16),
            pltpu.VMEM((2, hidden_width // parts, width), BF16),
            pltpu.VMEM((width // parts, hidden_width), BF16),
            pltpu.VMEM((hidden_width // parts, width), BF16),
            pltpu.VMEM((2, hidden_width), F32),
            pltpu.VMEM((2, width), F32),
            *[pltpu.VMEM((1, hidden_width), F32)] * 3,
            *[pltpu.VMEM((1, width), F32)] * 3,
            dma((1,)), dma((BATCHES,)), dma((1,)), dma((BATCHES,)), dma((2,)),
            dma((2,)), dma((2, units)), dma((2,)), dma((units,)),
            dma((3, 2)), dma((2, 2)), dma((2, units, 2)), dma((2, 2)), dma((2, 3)), dma((2, 3)),
        ],
        compiler_params=pltpu.CompilerParams(
            collective_id=0, has_side_effects=True, vmem_limit_bytes=60 << 20),
    )(tokens, tangent, bucket, mod_table.transpose(1, 0, 2), mod_rate.transpose(1, 0, 2), router.T, routes.T,
      w_in, b_in, w_out, b_out))


def solution(mesh):
    in_specs = (
        P(("dp", "seq"), None),
        P(("dp", "seq"), None),
        P("dp"),
        P(),
        P(),
        P(),
        P(("dp", "seq"), None),
        P("seq", None, None),
        P("seq", None),
        P("seq", None, None),
        P("seq", None),
    )
    out_specs = (P(("dp", "seq"), None), P(("dp", "seq"), None))
    return jax.shard_map(local, mesh=mesh, in_specs=in_specs, out_specs=out_specs, check_vma=False)
```

```python
import jax
import jax.numpy as jnp
from jax import lax
from jax.experimental import pallas as pl
from jax.experimental.pallas import tpu as pltpu
from jax.sharding import PartitionSpec as P

norm_eps = 1e-06
gelu_scale = 0.7978845608
cubic_coef = 0.044715

MESH = pl.DeviceIdType.MESH
F32 = jnp.float32
BF16 = jnp.bfloat16

X, Y, Z = 4, 4, 8
SIZES = (12, 8, 8, 4)
FIRST = (0, 12, 20, 28)
SLOTS = 32
SEND_ORDER = (0, 1, 3, 2)
HELD_BACK = (3, 2)
WORK_ORDER = (1, 2, 3)
CHUNKS = 2
WINDOW = 2
EARLY = 3
TOKENS_AT = 3
UP, DOWN = 0, 1


def wait_bytes(ref, sem):
    pltpu.make_async_copy(ref, ref, sem).wait()


def kernel(
    tok, tan, bucket, table, rate, router, routes_t, w_in, b_in, w_out, b_out,
    out, out_tan,
    modded, modded_tan, tx, rx, back, acc, mix_hi, mix_lo, hid, mods, wbi, wbo, near_in, near_out,
    bias_in, bias_out, bi_up, bi_down, bo_up, bo_down,
    send_sem, recv_sem, ret_send, ret_recv, own_sem, near_send, near_recv,
    spread_send, rest_sem, first_sem, pass_send, bias_send, bias_recv,
):
    rows, width = tok.shape
    cap = tx.shape[1] // 2
    hidden_width = wbi.shape[2]
    dp, seq = lax.axis_index("dp"), lax.axis_index("seq")
    y, core = dp // 2, dp % 2
    x, z = seq // Z, seq % Z

    def device(dy, c, to_x, dz):
        return {"dp": ((y + dy + Y) % Y) * 2 + c, "seq": to_x * Z + (z + dz + Z) % Z}

    def remote(src, dst, send, recv, to):
        return pltpu.make_async_remote_copy(src, dst, send, recv, device_id=to, device_id_type=MESH)

    barrier = pltpu.get_barrier_semaphore()
    peers = [
        device(0, (core + dc) % 2, (x + dx) % X, dz)
        for dz in (0, 1, -1, 2, -2) for dx in range(X) for dc in range(2)
        if (dz, dx, dc) != (0, 0, 0)
    ]
    peers += [device(dy, c, x, 0) for dy in (1, -1) for c in range(2)]
    for peer in peers:
        pl.semaphore_signal(barrier, inc=1, device_id=peer, device_id_type=MESH)
    pl.semaphore_wait(barrier, len(peers))

    part = (near_in.shape[1], near_out.shape[1])
    step = (part[0] // CHUNKS, part[1] // CHUNKS)
    units = [(a, k) for a in range(2) for k in range(CHUNKS)]
    near, full, held = (near_in, near_out), (w_in, w_out), (wbi, wbo)

    def near_copy(a, k, kind):
        return remote(
            full[a].at[0, pl.ds(dp * part[a] + k * step[a], step[a])],
            near[a].at[kind, pl.ds(k * step[a], step[a])],
            near_send.at[a], near_recv.at[kind, a * CHUNKS + k],
            device(0, core, x, -2 if kind == UP else 2))

    biases = []
    for kind, dz, to_in, to_out in ((UP, -2, bi_up, bo_up), (DOWN, 2, bi_down, bo_down)):
        to = device(0, core, x, dz)
        biases.append(remote(b_in, to_in, bias_send.at[0, kind], bias_recv.at[0, kind], to))
        biases.append(remote(b_out, to_out, bias_send.at[1, kind], bias_recv.at[1, kind], to))
    for a, k in units[:WINDOW]:
        for kind in (UP, DOWN):
            near_copy(a, k, kind).start()
    for copy in biases:
        copy.start()

    pltpu.make_async_copy(w_in.at[0], wbi.at[0], own_sem.at[0]).start()
    pltpu.make_async_copy(w_out.at[0], wbo.at[0], own_sem.at[1]).start()

    at_row = lax.broadcasted_iota(jnp.int32, (table.shape[1], width), 0) == bucket[0]
    for k in range(3):
        for first, source in ((0, table), (3, rate)):
            mods[pl.ds(first + k, 1)] = jnp.sum(
                jnp.where(at_row, source[k].astype(F32), 0.0), axis=0, keepdims=True)
    offset, offset_tan = mods[pl.ds(0, 1)], mods[pl.ds(3, 1)]
    scale, scale_tan = 1.0 + mods[pl.ds(1, 1)], mods[pl.ds(4, 1)]

    @pl.loop(0, rows // 16)
    def _(i):
        at = pl.ds(pl.multiple_of(i * 16, 16), 16)
        values = tok[at].astype(F32)
        deltas = tan[at].astype(F32)
        center = values - jnp.mean(values, axis=-1, keepdims=True)
        spread = jnp.mean(center * center, axis=-1, keepdims=True)
        inverse = lax.rsqrt(spread + norm_eps)
        normed = center * inverse
        normed_tan = (
            deltas
            - jnp.mean(deltas, axis=-1, keepdims=True)
            - normed * jnp.mean(normed * deltas, axis=-1, keepdims=True)
        ) * inverse
        modded[at] = (normed * scale + offset).astype(BF16)
        modded_tan[at] = (normed_tan * scale + normed * scale_tan + offset_tan).astype(BF16)

    def expert_of(block, batch):
        if batch == 0:
            to_x, move = block % X, block // X - 3 * (block // (2 * X))
        elif batch == 3:
            to_x, move = block, 4
        else:
            to_x, move = block // 2, (batch + 1) * (1 - 2 * (block % 2))
        return to_x * Z + (z + move + Z) % Z

    def out_legs(batch):
        first = FIRST[batch]
        for dx in range(X):
            to_x = (x + dx) % X
            if batch == 0:
                for k, dz in enumerate((0, 1, -1)):
                    yield first + k * X + to_x, first + k * X + x, device(0, core, to_x, dz), (dx, k) == (0, 0)
            elif batch == 3:
                side = dx % 2
                yield first + to_x, first + x // 2 * 2 + core, device(0, side, to_x, 2 - 4 * side), False
            else:
                for c in range(2):
                    side = (core + c) % 2
                    dz = (batch - 1) * (1 - 2 * side)
                    yield (first + to_x * 2 + side, first + x * 2 + core, device(0, side, to_x, dz),
                           (batch, dx, c) == (1, 0, 0))

    def home_legs(batch):
        first = FIRST[batch]
        sign = 1 - 2 * core
        if batch == 3:
            for h in range(2):
                to_x = 2 * h + (x + core) % 2
                for c in range(2):
                    yield first + 2 * h + c, first + x, device(0, c, to_x, -2 * sign), False
            return
        for dx in range(X):
            to_x = (x + dx) % X
            if batch == 0:
                for k, dz in enumerate((0, 1, -1)):
                    yield first + k * X + to_x, first + k * X + x, device(0, core, to_x, -dz), (dx, k) == (0, 0)
            else:
                for c in range(2):
                    side = (core + c) % 2
                    yield (first + to_x * 2 + side, first + x * 2 + core,
                           device(0, side, to_x, -(batch - 1) * sign), (batch, dx, c) == (1, 0, 0))

    def send_out(batch):
        for here, there, to, own in out_legs(batch):
            if own:
                pltpu.make_async_copy(tx.at[here], rx.at[there], recv_sem.at[batch]).start()
            else:
                remote(tx.at[here], rx.at[there], send_sem.at[0], recv_sem.at[batch], to).start()

    one_t, two_t = routes_t[0:1], routes_t[1:2]
    square = (rows, rows)
    down, across = lax.broadcasted_iota(jnp.int32, square, 0), lax.broadcasted_iota(jnp.int32, square, 1)
    early = (down < across).astype(F32).astype(BF16)
    late = (across < down).astype(F32).astype(BF16)
    for batch in SEND_ORDER:
        size = SIZES[batch]
        line = lax.broadcasted_iota(jnp.int32, (size * cap, rows), 0)
        expert = expert_of(line // cap, batch)
        named = (one_t == expert) | (two_t == expert)
        rank = jnp.dot(named.astype(F32).astype(BF16), early, preferred_element_type=F32)
        pick = (named & (rank == (line % cap).astype(F32))).astype(F32).astype(BF16)

        @pl.loop(0, width // 512)
        def _(n, batch=batch, size=size, pick=pick):
            cols = pl.ds(pl.multiple_of(n * 512, 512), 512)
            for source, first in ((modded, 0), (modded_tan, cap)):
                packed = jnp.dot(pick, source[:, cols], preferred_element_type=F32).astype(BF16)
                tx[pl.ds(FIRST[batch], size), pl.ds(first, cap), cols] = packed.reshape(size, cap, 512)

        if batch not in HELD_BACK:
            send_out(batch)

    turn = (((1,), (1,)), ((), ()))
    logits = lax.dot_general(modded[...], router[...], turn, preferred_element_type=F32)
    logit_tan = lax.dot_general(modded_tan[...], router[...], turn, preferred_element_type=F32)
    one = jnp.sum(jnp.where(down == across, one_t, 0).astype(F32), axis=1, keepdims=True).astype(jnp.int32)
    second = jnp.sum(jnp.where(down == across, two_t, 0).astype(F32), axis=1, keepdims=True).astype(jnp.int32)
    lane = lax.broadcasted_iota(jnp.int32, logits.shape, 1)

    def gap(values):
        return jnp.sum(jnp.where(lane == one, values, 0.0), axis=1, keepdims=True) - jnp.sum(
            jnp.where(lane == second, values, 0.0), axis=1, keepdims=True)

    weight = 1.0 / (1.0 + jnp.exp(-gap(logits)))
    weight_tan = weight * (1.0 - weight) * gap(logit_tan)
    for batch, size in enumerate(SIZES):
        spot = lax.broadcasted_iota(jnp.int32, (rows, size * 2 * cap), 1)
        cols = pl.ds(FIRST[batch] * 2 * cap, size * 2 * cap)
        expert = expert_of(spot // (2 * cap), batch)
        is_one, is_two = one == expert, second == expert
        named = is_one | is_two
        rank = jnp.dot(late, named.astype(F32).astype(BF16), preferred_element_type=F32)
        chosen = named & (rank == (spot % cap).astype(F32))
        is_main = (spot % (2 * cap)) < cap
        share = jnp.where(is_one, weight, 1.0 - weight)
        share_tan = jnp.where(is_one, weight_tan, -weight_tan)
        for first, value in (
            (0, jnp.where(chosen & is_main, share, 0.0)),
            (rows, jnp.where(chosen, jnp.where(is_main, share_tan, share), 0.0)),
        ):
            high = value.astype(BF16)
            mix_hi[pl.ds(first, rows), cols] = high
            mix_lo[pl.ds(first, rows), cols] = (value - high.astype(F32)).astype(BF16)

    def spread_weights(a, k, kind):
        src = near[a].at[kind, pl.ds(k * step[a], step[a])]
        dst = held[a].at[1, pl.ds(dp * part[a] + k * step[a], step[a])]
        unit = a * CHUNKS + k
        send, rest = spread_send.at[kind, a], rest_sem.at[a]

        @pl.when(core == kind)
        def _():
            pltpu.make_async_copy(src, dst, rest).start()

        @pl.when(core != kind)
        def _():
            remote(src, dst, send, rest, device(0, kind, x, 0)).start()

        @pl.when(core == 0)
        def _():
            remote(src, dst, send, first_sem.at[unit, 0], device(1, kind, x, 0)).start()
            remote(src, dst, send, rest, device(-1, kind, x, 0)).start()

        @pl.when(core == 1)
        def _():
            remote(src, dst, send, rest, device(1, kind, x, 0)).start()
            remote(src, dst, send, first_sem.at[unit, 1], device(-1, kind, x, 0)).start()

    def pass_weights(a, k):
        for side, dy in ((0, 1), (1, -1)):
            piece = ((y - dy + Y) % Y) * 2 + side
            ref = held[a].at[1, pl.ds(piece * part[a] + k * step[a], step[a])]
            wait_bytes(ref, first_sem.at[a * CHUNKS + k, side])
            remote(ref, ref, pass_send.at[a], rest_sem.at[a], device(dy, core, x, 0)).start()

    def work(batch):
        place, size = min(batch, 1), SIZES[batch]
        span = size * 2 * cap
        blocks = pl.ds(FIRST[batch], size)
        wait_bytes(rx.at[blocks], recv_sem.at[batch])

        @pl.loop(0, hidden_width // 256)
        def _(n):
            cols = pl.ds(pl.multiple_of(n * 256, 256), 256)
            both = jnp.dot(
                rx[blocks].reshape(span, width), wbi[place, :, cols], preferred_element_type=F32
            ).reshape(size, 2 * cap, 256)
            hidden = both[:, :cap] + bias_in[pl.ds(place, 1), cols].reshape(1, 1, 256)
            hidden_tan = both[:, cap:]
            tanh_val = jnp.tanh(gelu_scale * (hidden + cubic_coef * hidden * hidden * hidden))
            hid[pl.ds(0, size), pl.ds(0, cap), cols] = (0.5 * hidden * (1.0 + tanh_val)).astype(BF16)
            slope = 0.5 * (1.0 + tanh_val) + 0.5 * hidden * (1.0 - tanh_val * tanh_val) * gelu_scale * (
                1.0 + 3.0 * cubic_coef * hidden * hidden
            )
            hid[pl.ds(0, size), pl.ds(cap, cap), cols] = (slope * hidden_tan).astype(BF16)

        @pl.loop(0, width // 512)
        def _(n):
            cols = pl.ds(pl.multiple_of(n * 512, 512), 512)
            both = jnp.dot(
                hid[pl.ds(0, size)].reshape(span, hidden_width), wbo[place, :, cols], preferred_element_type=F32
            ).reshape(size, 2 * cap, 512)
            rx[blocks, pl.ds(0, cap), cols] = (
                both[:, :cap] + bias_out[pl.ds(place, 1), cols].reshape(1, 1, 512)).astype(BF16)
            rx[blocks, pl.ds(cap, cap), cols] = both[:, cap:].astype(BF16)

        for here, there, to, own in home_legs(batch):
            if own:
                pltpu.make_async_copy(rx.at[here], back.at[there], ret_recv.at[batch]).start()
            else:
                remote(rx.at[here], back.at[there], ret_send.at[0], ret_recv.at[batch], to).start()

    for copy in biases:
        copy.wait()
    for bias, own, up, low in ((bias_in, b_in, bi_up, bi_down), (bias_out, b_out, bo_up, bo_down)):
        bias[pl.ds(0, 1)] = own[...]
        bias[pl.ds(1, 1)] = jnp.where(core == 0, up[...], low[...])

    def own_work():
        wait_bytes(wbi.at[0], own_sem.at[0])
        wait_bytes(wbo.at[0], own_sem.at[1])
        work(0)

    for u, (a, k) in enumerate(units):
        for kind in (UP, DOWN):
            near_copy(a, k, kind).wait_recv()
        if u + WINDOW < len(units):
            for kind in (UP, DOWN):
                near_copy(*units[u + WINDOW], kind).start()
        for kind in (UP, DOWN):
            spread_weights(a, k, kind)
        if u == TOKENS_AT:
            for batch in HELD_BACK:
                send_out(batch)
        if u > 0:
            pass_weights(*units[u - 1])
        if u == EARLY:
            own_work()
    pass_weights(*units[-1])
    if EARLY >= len(units):
        own_work()
    for a in range(2):
        wait_bytes(held[a].at[1, pl.ds(0, 6 * part[a])], rest_sem.at[a])
    for batch in WORK_ORDER:
        work(batch)

    for order, batch in enumerate((0,) + WORK_ORDER):
        blocks = pl.ds(FIRST[batch], SIZES[batch])
        wait_bytes(back.at[blocks], ret_recv.at[batch])
        span = SIZES[batch] * 2 * cap
        spots = pl.ds(FIRST[batch] * 2 * cap, span)

        @pl.loop(0, width // 512)
        def _(n, order=order, blocks=blocks, span=span, spots=spots):
            cols = pl.ds(pl.multiple_of(n * 512, 512), 512)
            parts = back[blocks, :, cols].reshape(span, 512)
            mixed = jnp.dot(mix_hi[:, spots], parts, preferred_element_type=F32) + jnp.dot(
                mix_lo[:, spots], parts, preferred_element_type=F32)
            if order > 0:
                mixed = mixed + acc[:, cols]
            if order < len(WORK_ORDER):
                acc[:, cols] = mixed
            else:
                gate, gate_tan = mods[pl.ds(2, 1), cols], mods[pl.ds(5, 1), cols]
                mixture, mixture_tan = mixed[:rows], mixed[rows:]
                out[:, cols] = (tok[:, cols].astype(F32) + gate * mixture).astype(BF16)
                out_tan[:, cols] = (
                    tan[:, cols].astype(F32) + gate_tan * mixture + gate * mixture_tan).astype(BF16)

    wait_bytes(tx.at[pl.ds(0, SLOTS - 2)], send_sem.at[0])
    wait_bytes(rx.at[pl.ds(0, SLOTS - 2)], ret_send.at[0])
    for a in range(2):
        wait_bytes(held[a].at[0, pl.ds(0, 2 * part[a])], near_send.at[a])
        for kind in (UP, DOWN):
            @pl.when(core == kind)
            def _(a=a, kind=kind):
                wait_bytes(held[a].at[0, pl.ds(0, 2 * part[a])], spread_send.at[kind, a])

            @pl.when(core != kind)
            def _(a=a, kind=kind):
                wait_bytes(held[a].at[0, pl.ds(0, 3 * part[a])], spread_send.at[kind, a])

        wait_bytes(held[a].at[0, pl.ds(0, 2 * part[a])], pass_send.at[a])


def local(tokens, tangent, bucket, mod_table, mod_rate, router, routes, w_in, b_in, w_out, b_out):
    rows, width = tokens.shape
    hidden_width = w_in.shape[2]
    cap = 4 * rows // router.shape[1]
    parts = lax.axis_size("dp")
    vmem = pl.BlockSpec(memory_space=pltpu.VMEM)
    smem = pl.BlockSpec(memory_space=pltpu.SMEM)
    hbm = pl.BlockSpec(memory_space=pl.ANY)
    shape = jax.ShapeDtypeStruct((rows, width), BF16)
    dma = pltpu.SemaphoreType.DMA
    units = 2 * CHUNKS
    blocks = pltpu.VMEM((SLOTS, 2 * cap, width), BF16)
    mix = pltpu.VMEM((2 * rows, SLOTS * 2 * cap), BF16)
    return tuple(pl.pallas_call(
        kernel,
        out_shape=(shape, shape),
        in_specs=[vmem, vmem, smem, vmem, vmem, vmem, vmem, hbm, vmem, hbm, vmem],
        out_specs=(vmem, vmem),
        scratch_shapes=[
            pltpu.VMEM((rows, width), BF16),
            pltpu.VMEM((rows, width), BF16),
            blocks, blocks, blocks,
            pltpu.VMEM((2 * rows, width), F32),
            mix, mix,
            pltpu.VMEM((max(SIZES), 2 * cap, hidden_width), BF16),
            pltpu.VMEM((8, width), F32),
            pltpu.VMEM((2, width, hidden_width), BF16),
            pltpu.VMEM((2, hidden_width, width), BF16),
            pltpu.VMEM((2, width // parts, hidden_width), BF16),
            pltpu.VMEM((2, hidden_width // parts, width), BF16),
            pltpu.VMEM((2, hidden_width), F32),
            pltpu.VMEM((2, width), F32),
            *[pltpu.VMEM((1, hidden_width), F32)] * 2,
            *[pltpu.VMEM((1, width), F32)] * 2,
            dma((1,)), dma((len(SIZES),)), dma((1,)), dma((len(SIZES),)), dma((2,)),
            dma((2,)), dma((2, units)),
            dma((2, 2)), dma((2,)), dma((units, 2)), dma((2,)), dma((2, 2)), dma((2, 2)),
        ],
        compiler_params=pltpu.CompilerParams(
            collective_id=0, has_side_effects=True, vmem_limit_bytes=60 << 20),
    )(tokens, tangent, bucket, mod_table.transpose(1, 0, 2), mod_rate.transpose(1, 0, 2), router.T, routes.T,
      w_in, b_in, w_out, b_out))


def solution(mesh):
    in_specs = (
        P(("dp", "seq"), None),
        P(("dp", "seq"), None),
        P("dp"),
        P(),
        P(),
        P(),
        P(("dp", "seq"), None),
        P("seq", None, None),
        P("seq", None),
        P("seq", None, None),
        P("seq", None),
    )
    out_specs = (P(("dp", "seq"), None), P(("dp", "seq"), None))
    return jax.shard_map(local, mesh=mesh, in_specs=in_specs, out_specs=out_specs, check_vma=False)
```

```python
import jax
import jax.numpy as jnp
from jax import lax
from jax.experimental import pallas as pl
from jax.experimental.pallas import tpu as pltpu
from jax.sharding import PartitionSpec as P

norm_eps = 1e-06
gelu_scale = 0.7978845608
cubic_coef = 0.044715

MESH = pl.DeviceIdType.MESH
F32 = jnp.float32
BF16 = jnp.bfloat16

X, Y, Z = 4, 4, 8
SIZES = (12, 8, 8, 4)
FIRST = (0, 12, 20, 28)
SLOTS = 32
WORK_ORDER = (1, 2, 3)
CHUNKS = 2
WINDOW = 2
EARLY = 3
RELAY_AT = 1
UP, DOWN = 0, 1


def wait_bytes(ref, sem):
    pltpu.make_async_copy(ref, ref, sem).wait()


def kernel(
    tok, tan, bucket, table, rate, router, routes_t, w_in, b_in, w_out, b_out,
    out, out_tan,
    modded, modded_tan, around, routes_around, tx, rx, back, acc, mix_hi, mix_lo, hid, mods, wbi, wbo, near_in, near_out,
    bias_in, bias_out, bi_up, bi_down, bo_up, bo_down,
    send_sem, recv_sem, ret_send, ret_recv, own_sem, near_send, near_recv,
    around_send, around_recv, routes_recv, spread_send, rest_sem, first_sem, pass_send, bias_send, bias_recv,
):
    rows, width = tok.shape
    cap = tx.shape[1] // 2
    hidden_width = wbi.shape[2]
    dp, seq = lax.axis_index("dp"), lax.axis_index("seq")
    y, core = dp // 2, dp % 2
    x, z = seq // Z, seq % Z

    def device(dy, c, to_x, dz):
        return {"dp": ((y + dy + Y) % Y) * 2 + c, "seq": to_x * Z + (z + dz + Z) % Z}

    def remote(src, dst, send, recv, to):
        return pltpu.make_async_remote_copy(src, dst, send, recv, device_id=to, device_id_type=MESH)

    barrier = pltpu.get_barrier_semaphore()
    peers = [
        device(0, (core + dc) % 2, (x + dx) % X, dz)
        for dz in (0, 1, -1, 2, -2) for dx in range(X) for dc in range(2)
        if (dz, dx, dc) != (0, 0, 0)
    ]
    peers += [device(dy, c, x, 0) for dy in (1, -1) for c in range(2)]
    for peer in peers:
        pl.semaphore_signal(barrier, inc=1, device_id=peer, device_id_type=MESH)
    pl.semaphore_wait(barrier, len(peers))

    part = (near_in.shape[1], near_out.shape[1])
    step = (part[0] // CHUNKS, part[1] // CHUNKS)
    units = [(a, k) for a in range(2) for k in range(CHUNKS)]
    near, full, held = (near_in, near_out), (w_in, w_out), (wbi, wbo)

    def near_copy(a, k, kind):
        return remote(
            full[a].at[0, pl.ds(dp * part[a] + k * step[a], step[a])],
            near[a].at[kind, pl.ds(k * step[a], step[a])],
            near_send.at[a], near_recv.at[kind, a * CHUNKS + k],
            device(0, core, x, -2 if kind == UP else 2))

    biases = []
    for kind, dz, to_in, to_out in ((UP, -2, bi_up, bo_up), (DOWN, 2, bi_down, bo_down)):
        to = device(0, core, x, dz)
        biases.append(remote(b_in, to_in, bias_send.at[0, kind], bias_recv.at[0, kind], to))
        biases.append(remote(b_out, to_out, bias_send.at[1, kind], bias_recv.at[1, kind], to))
    for a, k in units[:WINDOW]:
        for kind in (UP, DOWN):
            near_copy(a, k, kind).start()
    route_copies = [
        remote(routes_t, routes_around.at[side], around_send.at[1 + side], routes_recv.at[side], device(0, core, x, dz))
        for side, dz in ((0, 1), (1, -1))
    ]
    for copy in biases + route_copies:
        copy.start()

    pltpu.make_async_copy(w_in.at[0], wbi.at[0], own_sem.at[0]).start()
    pltpu.make_async_copy(w_out.at[0], wbo.at[0], own_sem.at[1]).start()

    at_row = lax.broadcasted_iota(jnp.int32, (table.shape[1], width), 0) == bucket[0]
    for k in range(3):
        for first, source in ((0, table), (3, rate)):
            mods[pl.ds(first + k, 1)] = jnp.sum(
                jnp.where(at_row, source[k].astype(F32), 0.0), axis=0, keepdims=True)
    offset, offset_tan = mods[pl.ds(0, 1)], mods[pl.ds(3, 1)]
    scale, scale_tan = 1.0 + mods[pl.ds(1, 1)], mods[pl.ds(4, 1)]

    @pl.loop(0, rows // 16)
    def _(i):
        at = pl.ds(pl.multiple_of(i * 16, 16), 16)
        values = tok[at].astype(F32)
        deltas = tan[at].astype(F32)
        center = values - jnp.mean(values, axis=-1, keepdims=True)
        spread = jnp.mean(center * center, axis=-1, keepdims=True)
        inverse = lax.rsqrt(spread + norm_eps)
        normed = center * inverse
        normed_tan = (
            deltas
            - jnp.mean(deltas, axis=-1, keepdims=True)
            - normed * jnp.mean(normed * deltas, axis=-1, keepdims=True)
        ) * inverse
        modded[at] = (normed * scale + offset).astype(BF16)
        modded_tan[at] = (normed_tan * scale + normed * scale_tan + offset_tan).astype(BF16)

    def expert_of(block, batch):
        if batch == 0:
            to_x, move = block % X, block // X - 3 * (block // (2 * X))
        elif batch == 3:
            to_x, move = block, 4
        else:
            to_x, move = block // 2, (batch + 1) * (1 - 2 * (block % 2))
        return to_x * Z + (z + move + Z) % Z

    def out_legs(batch, parts):
        first = FIRST[batch]
        for dx in range(X):
            to_x = (x + dx) % X
            if batch == 0:
                for k in range(3):
                    if k in parts:
                        yield first + k * X + to_x, first + k * X + x, device(0, core, to_x, 0), dx == 0
            elif batch == 3:
                side = dx % 2
                yield first + to_x, first + x // 2 * 2 + core, device(0, side, to_x, 1 - 2 * side), False
            else:
                for c in range(2):
                    side = (core + c) % 2
                    yield (first + to_x * 2 + side, first + x * 2 + core, device(0, side, to_x, 0),
                           (dx, c) == (0, 0))

    def home_legs(batch):
        first = FIRST[batch]
        sign = 1 - 2 * core
        if batch == 3:
            for h in range(2):
                to_x = 2 * h + (x + core) % 2
                for c in range(2):
                    yield first + 2 * h + c, first + x, device(0, c, to_x, -2 * sign), False
            return
        for dx in range(X):
            to_x = (x + dx) % X
            if batch == 0:
                for k, dz in enumerate((0, 1, -1)):
                    yield first + k * X + to_x, first + k * X + x, device(0, core, to_x, -dz), (dx, k) == (0, 0)
            else:
                for c in range(2):
                    side = (core + c) % 2
                    yield (first + to_x * 2 + side, first + x * 2 + core,
                           device(0, side, to_x, -(batch - 1) * sign), (batch, dx, c) == (1, 0, 0))

    def send_out(batch, parts=()):
        for here, there, to, own in out_legs(batch, parts):
            if own:
                pltpu.make_async_copy(tx.at[here], rx.at[there], recv_sem.at[batch]).start()
            else:
                remote(tx.at[here], rx.at[there], send_sem.at[0], recv_sem.at[batch], to).start()

    square = (rows, rows)
    down, across = lax.broadcasted_iota(jnp.int32, square, 0), lax.broadcasted_iota(jnp.int32, square, 1)
    early = (down < across).astype(F32).astype(BF16)
    late = (across < down).astype(F32).astype(BF16)
    one_t, two_t = routes_t[0:1], routes_t[1:2]

    def pack(count, move, to_x_of, slot_of, who):
        if who == 0:
            main, tan_rows, first, second = modded, modded_tan, one_t, two_t
        else:
            main, tan_rows = around.at[who - 1, 0], around.at[who - 1, 1]
            first, second = routes_around[who - 1, 0:1], routes_around[who - 1, 1:2]
        line = lax.broadcasted_iota(jnp.int32, (count * cap, rows), 0)
        base = (0, -1, 1)[who]
        expert = to_x_of(line // cap) * Z + (z + base + move(line // cap) + Z) % Z
        named = (first == expert) | (second == expert)
        rank = jnp.dot(named.astype(F32).astype(BF16), early, preferred_element_type=F32)
        pick = (named & (rank == (line % cap).astype(F32))).astype(F32).astype(BF16)

        @pl.loop(0, width // 512)
        def _(n):
            cols = pl.ds(pl.multiple_of(n * 512, 512), 512)
            for source, at in ((main, 0), (tan_rows, cap)):
                packed = jnp.dot(pick, source[:, cols], preferred_element_type=F32).astype(BF16)
                packed = packed.reshape(count, cap, 512)
                for start, size, slot in slot_of:
                    tx[pl.ds(slot, size), pl.ds(at, cap), cols] = packed[start:start + size]

    around_copies = []
    for side, dz in ((0, 1), (1, -1)):
        to = device(0, core, x, dz)
        for j, source in enumerate((modded, modded_tan)):
            around_copies.append(
                remote(source, around.at[side, j], around_send.at[0], around_recv.at[side], to))
    for copy in around_copies:
        copy.start()

    pack(4, lambda b: 0 * b, lambda b: b, [(0, 4, 0)], 0)
    send_out(0, (0,))
    pack(8, lambda b: 2 - 4 * (b % 2), lambda b: b // 2, [(0, 8, FIRST[1])], 0)
    send_out(1)

    def pack_around():
        for copy in route_copies:
            copy.wait()
        for side in range(2):
            wait_bytes(around.at[side], around_recv.at[side])
            up = 1 - 2 * side
            odd = (x + side) % 2
            pack(
                10, lambda b: up * jnp.where(b < 4, 1, jnp.where(b < 8, 3, 4)),
                lambda b: jnp.where(b < 8, b % X, 2 * (b - 8) + odd),
                [(0, 4, 4 + 4 * side)] + [(4 + j, 1, FIRST[2] + 2 * j + side) for j in range(4)]
                + [(8 + j, 1, FIRST[3] + 2 * j + odd) for j in range(2)], 1 + side)
        send_out(0, (1, 2))
        send_out(3)
        send_out(2)

    turn = (((1,), (1,)), ((), ()))
    logits = lax.dot_general(modded[...], router[...], turn, preferred_element_type=F32)
    logit_tan = lax.dot_general(modded_tan[...], router[...], turn, preferred_element_type=F32)
    one = jnp.sum(jnp.where(down == across, one_t, 0).astype(F32), axis=1, keepdims=True).astype(jnp.int32)
    second = jnp.sum(jnp.where(down == across, two_t, 0).astype(F32), axis=1, keepdims=True).astype(jnp.int32)
    lane = lax.broadcasted_iota(jnp.int32, logits.shape, 1)

    def gap(values):
        return jnp.sum(jnp.where(lane == one, values, 0.0), axis=1, keepdims=True) - jnp.sum(
            jnp.where(lane == second, values, 0.0), axis=1, keepdims=True)

    weight = 1.0 / (1.0 + jnp.exp(-gap(logits)))
    weight_tan = weight * (1.0 - weight) * gap(logit_tan)
    for batch, size in enumerate(SIZES):
        spot = lax.broadcasted_iota(jnp.int32, (rows, size * 2 * cap), 1)
        cols = pl.ds(FIRST[batch] * 2 * cap, size * 2 * cap)
        expert = expert_of(spot // (2 * cap), batch)
        is_one, is_two = one == expert, second == expert
        named = is_one | is_two
        rank = jnp.dot(late, named.astype(F32).astype(BF16), preferred_element_type=F32)
        chosen = named & (rank == (spot % cap).astype(F32))
        is_main = (spot % (2 * cap)) < cap
        share = jnp.where(is_one, weight, 1.0 - weight)
        share_tan = jnp.where(is_one, weight_tan, -weight_tan)
        for first, value in (
            (0, jnp.where(chosen & is_main, share, 0.0)),
            (rows, jnp.where(chosen, jnp.where(is_main, share_tan, share), 0.0)),
        ):
            high = value.astype(BF16)
            mix_hi[pl.ds(first, rows), cols] = high
            mix_lo[pl.ds(first, rows), cols] = (value - high.astype(F32)).astype(BF16)

    def spread_weights(a, k, kind):
        src = near[a].at[kind, pl.ds(k * step[a], step[a])]
        dst = held[a].at[1, pl.ds(dp * part[a] + k * step[a], step[a])]
        unit = a * CHUNKS + k
        send, rest = spread_send.at[kind, a], rest_sem.at[a]

        @pl.when(core == kind)
        def _():
            pltpu.make_async_copy(src, dst, rest).start()

        @pl.when(core != kind)
        def _():
            remote(src, dst, send, rest, device(0, kind, x, 0)).start()

        @pl.when(core == 0)
        def _():
            remote(src, dst, send, first_sem.at[unit, 0], device(1, kind, x, 0)).start()
            remote(src, dst, send, rest, device(-1, kind, x, 0)).start()

        @pl.when(core == 1)
        def _():
            remote(src, dst, send, rest, device(1, kind, x, 0)).start()
            remote(src, dst, send, first_sem.at[unit, 1], device(-1, kind, x, 0)).start()

    def pass_weights(a, k):
        for side, dy in ((0, 1), (1, -1)):
            piece = ((y - dy + Y) % Y) * 2 + side
            ref = held[a].at[1, pl.ds(piece * part[a] + k * step[a], step[a])]
            wait_bytes(ref, first_sem.at[a * CHUNKS + k, side])
            remote(ref, ref, pass_send.at[a], rest_sem.at[a], device(dy, core, x, 0)).start()

    def work(batch):
        place, size = min(batch, 1), SIZES[batch]
        span = size * 2 * cap
        blocks = pl.ds(FIRST[batch], size)
        wait_bytes(rx.at[blocks], recv_sem.at[batch])

        @pl.loop(0, hidden_width // 256)
        def _(n):
            cols = pl.ds(pl.multiple_of(n * 256, 256), 256)
            both = jnp.dot(
                rx[blocks].reshape(span, width), wbi[place, :, cols], preferred_element_type=F32
            ).reshape(size, 2 * cap, 256)
            hidden = both[:, :cap] + bias_in[pl.ds(place, 1), cols].reshape(1, 1, 256)
            hidden_tan = both[:, cap:]
            tanh_val = jnp.tanh(gelu_scale * (hidden + cubic_coef * hidden * hidden * hidden))
            hid[pl.ds(0, size), pl.ds(0, cap), cols] = (0.5 * hidden * (1.0 + tanh_val)).astype(BF16)
            slope = 0.5 * (1.0 + tanh_val) + 0.5 * hidden * (1.0 - tanh_val * tanh_val) * gelu_scale * (
                1.0 + 3.0 * cubic_coef * hidden * hidden
            )
            hid[pl.ds(0, size), pl.ds(cap, cap), cols] = (slope * hidden_tan).astype(BF16)

        @pl.loop(0, width // 512)
        def _(n):
            cols = pl.ds(pl.multiple_of(n * 512, 512), 512)
            both = jnp.dot(
                hid[pl.ds(0, size)].reshape(span, hidden_width), wbo[place, :, cols], preferred_element_type=F32
            ).reshape(size, 2 * cap, 512)
            rx[blocks, pl.ds(0, cap), cols] = (
                both[:, :cap] + bias_out[pl.ds(place, 1), cols].reshape(1, 1, 512)).astype(BF16)
            rx[blocks, pl.ds(cap, cap), cols] = both[:, cap:].astype(BF16)

        for here, there, to, own in home_legs(batch):
            if own:
                pltpu.make_async_copy(rx.at[here], back.at[there], ret_recv.at[batch]).start()
            else:
                remote(rx.at[here], back.at[there], ret_send.at[0], ret_recv.at[batch], to).start()

    for copy in biases:
        copy.wait()
    for bias, own, up, low in ((bias_in, b_in, bi_up, bi_down), (bias_out, b_out, bo_up, bo_down)):
        bias[pl.ds(0, 1)] = own[...]
        bias[pl.ds(1, 1)] = jnp.where(core == 0, up[...], low[...])

    def own_work():
        wait_bytes(wbi.at[0], own_sem.at[0])
        wait_bytes(wbo.at[0], own_sem.at[1])
        work(0)

    for u, (a, k) in enumerate(units):
        for kind in (UP, DOWN):
            near_copy(a, k, kind).wait_recv()
        if u + WINDOW < len(units):
            for kind in (UP, DOWN):
                near_copy(*units[u + WINDOW], kind).start()
        for kind in (UP, DOWN):
            spread_weights(a, k, kind)
        if u == RELAY_AT:
            pack_around()
        if u > 0:
            pass_weights(*units[u - 1])
        if u == EARLY:
            own_work()
    pass_weights(*units[-1])
    if EARLY >= len(units):
        own_work()
    for a in range(2):
        wait_bytes(held[a].at[1, pl.ds(0, 6 * part[a])], rest_sem.at[a])
    for batch in WORK_ORDER:
        work(batch)

    for order, batch in enumerate((0,) + WORK_ORDER):
        blocks = pl.ds(FIRST[batch], SIZES[batch])
        wait_bytes(back.at[blocks], ret_recv.at[batch])
        span = SIZES[batch] * 2 * cap
        spots = pl.ds(FIRST[batch] * 2 * cap, span)

        @pl.loop(0, width // 512)
        def _(n, order=order, blocks=blocks, span=span, spots=spots):
            cols = pl.ds(pl.multiple_of(n * 512, 512), 512)
            parts = back[blocks, :, cols].reshape(span, 512)
            mixed = jnp.dot(mix_hi[:, spots], parts, preferred_element_type=F32) + jnp.dot(
                mix_lo[:, spots], parts, preferred_element_type=F32)
            if order > 0:
                mixed = mixed + acc[:, cols]
            if order < len(WORK_ORDER):
                acc[:, cols] = mixed
            else:
                gate, gate_tan = mods[pl.ds(2, 1), cols], mods[pl.ds(5, 1), cols]
                mixture, mixture_tan = mixed[:rows], mixed[rows:]
                out[:, cols] = (tok[:, cols].astype(F32) + gate * mixture).astype(BF16)
                out_tan[:, cols] = (
                    tan[:, cols].astype(F32) + gate_tan * mixture + gate * mixture_tan).astype(BF16)

    wait_bytes(tx.at[pl.ds(0, SLOTS - 5)], send_sem.at[0])
    wait_bytes(around, around_send.at[0])
    wait_bytes(rx.at[pl.ds(0, SLOTS - 2)], ret_send.at[0])
    for a in range(2):
        wait_bytes(held[a].at[0, pl.ds(0, 2 * part[a])], near_send.at[a])
        for kind in (UP, DOWN):
            @pl.when(core == kind)
            def _(a=a, kind=kind):
                wait_bytes(held[a].at[0, pl.ds(0, 2 * part[a])], spread_send.at[kind, a])

            @pl.when(core != kind)
            def _(a=a, kind=kind):
                wait_bytes(held[a].at[0, pl.ds(0, 3 * part[a])], spread_send.at[kind, a])

        wait_bytes(held[a].at[0, pl.ds(0, 2 * part[a])], pass_send.at[a])


def local(tokens, tangent, bucket, mod_table, mod_rate, router, routes, w_in, b_in, w_out, b_out):
    rows, width = tokens.shape
    hidden_width = w_in.shape[2]
    cap = 4 * rows // router.shape[1]
    parts = lax.axis_size("dp")
    vmem = pl.BlockSpec(memory_space=pltpu.VMEM)
    smem = pl.BlockSpec(memory_space=pltpu.SMEM)
    hbm = pl.BlockSpec(memory_space=pl.ANY)
    shape = jax.ShapeDtypeStruct((rows, width), BF16)
    dma = pltpu.SemaphoreType.DMA
    units = 2 * CHUNKS
    blocks = pltpu.VMEM((SLOTS, 2 * cap, width), BF16)
    mix = pltpu.VMEM((2 * rows, SLOTS * 2 * cap), BF16)
    return tuple(pl.pallas_call(
        kernel,
        out_shape=(shape, shape),
        in_specs=[vmem, vmem, smem, vmem, vmem, vmem, vmem, hbm, vmem, hbm, vmem],
        out_specs=(vmem, vmem),
        scratch_shapes=[
            pltpu.VMEM((rows, width), BF16),
            pltpu.VMEM((rows, width), BF16),
            pltpu.VMEM((2, 2, rows, width), BF16),
            pltpu.VMEM((2, 2, rows), jnp.int32),
            blocks, blocks, blocks,
            pltpu.VMEM((2 * rows, width), F32),
            mix, mix,
            pltpu.VMEM((max(SIZES), 2 * cap, hidden_width), BF16),
            pltpu.VMEM((8, width), F32),
            pltpu.VMEM((2, width, hidden_width), BF16),
            pltpu.VMEM((2, hidden_width, width), BF16),
            pltpu.VMEM((2, width // parts, hidden_width), BF16),
            pltpu.VMEM((2, hidden_width // parts, width), BF16),
            pltpu.VMEM((2, hidden_width), F32),
            pltpu.VMEM((2, width), F32),
            *[pltpu.VMEM((1, hidden_width), F32)] * 2,
            *[pltpu.VMEM((1, width), F32)] * 2,
            dma((1,)), dma((len(SIZES),)), dma((1,)), dma((len(SIZES),)), dma((2,)),
            dma((2,)), dma((2, units)),
            dma((3,)), dma((2,)), dma((2,)),
            dma((2, 2)), dma((2,)), dma((units, 2)), dma((2,)), dma((2, 2)), dma((2, 2)),
        ],
        compiler_params=pltpu.CompilerParams(
            collective_id=0, has_side_effects=True, vmem_limit_bytes=60 << 20),
    )(tokens, tangent, bucket, mod_table.transpose(1, 0, 2), mod_rate.transpose(1, 0, 2), router.T, routes.T,
      w_in, b_in, w_out, b_out))


def solution(mesh):
    in_specs = (
        P(("dp", "seq"), None),
        P(("dp", "seq"), None),
        P("dp"),
        P(),
        P(),
        P(),
        P(("dp", "seq"), None),
        P("seq", None, None),
        P("seq", None),
        P("seq", None, None),
        P("seq", None),
    )
    out_specs = (P(("dp", "seq"), None), P(("dp", "seq"), None))
    return jax.shard_map(local, mesh=mesh, in_specs=in_specs, out_specs=out_specs, check_vma=False)
```

```python
import jax
import jax.numpy as jnp
from jax import lax
from jax.experimental import pallas as pl
from jax.experimental.pallas import tpu as pltpu
from jax.sharding import PartitionSpec as P

norm_eps = 1e-06
gelu_scale = 0.7978845608
cubic_coef = 0.044715

MESH = pl.DeviceIdType.MESH
F32 = jnp.float32
BF16 = jnp.bfloat16

X, Y, Z = 4, 4, 8
SIZES = (12, 8, 8, 4)
FIRST = (0, 12, 20, 28)
SLOTS = 32
WORK_ORDER = (3, 2, 1)
CHUNKS = 2
WINDOW = 2
EARLY = 3
RELAY_AT = 1
UP, DOWN = 0, 1


def wait_bytes(ref, sem):
    pltpu.make_async_copy(ref, ref, sem).wait()


def kernel(
    tok, tan, bucket, table, rate, router, routes_t, w_in, b_in, w_out, b_out,
    out, out_tan,
    modded, modded_tan, around, routes_around, tx, rx, back, acc, mix_hi, mix_lo, hid, mods, wbi, wbo, near_in, near_out,
    bias_in, bias_out, bi_up, bi_down, bo_up, bo_down,
    send_sem, recv_sem, ret_send, ret_recv, own_sem, near_send, near_recv,
    around_send, around_recv, routes_recv, spread_send, rest_sem, first_sem, pass_send, bias_send, bias_recv,
):
    rows, width = tok.shape
    cap = tx.shape[1] // 2
    hidden_width = wbi.shape[2]
    dp, seq = lax.axis_index("dp"), lax.axis_index("seq")
    y, core = dp // 2, dp % 2
    x, z = seq // Z, seq % Z

    def device(dy, c, to_x, dz):
        return {"dp": ((y + dy + Y) % Y) * 2 + c, "seq": to_x * Z + (z + dz + Z) % Z}

    def remote(src, dst, send, recv, to):
        return pltpu.make_async_remote_copy(src, dst, send, recv, device_id=to, device_id_type=MESH)

    barrier = pltpu.get_barrier_semaphore()
    peers = [
        device(0, (core + dc) % 2, (x + dx) % X, dz)
        for dz in (0, 1, -1, 2, -2) for dx in range(X) for dc in range(2)
        if (dz, dx, dc) != (0, 0, 0)
    ]
    peers += [device(dy, c, x, 0) for dy in (1, -1) for c in range(2)]
    for peer in peers:
        pl.semaphore_signal(barrier, inc=1, device_id=peer, device_id_type=MESH)
    pl.semaphore_wait(barrier, len(peers))

    part = (near_in.shape[1], near_out.shape[1])
    step = (part[0] // CHUNKS, part[1] // CHUNKS)
    units = [(a, k) for a in range(2) for k in range(CHUNKS)]
    near, full, held = (near_in, near_out), (w_in, w_out), (wbi, wbo)

    def near_copy(a, k, kind):
        return remote(
            full[a].at[0, pl.ds(dp * part[a] + k * step[a], step[a])],
            near[a].at[kind, pl.ds(k * step[a], step[a])],
            near_send.at[a], near_recv.at[kind, a * CHUNKS + k],
            device(0, core, x, -2 if kind == UP else 2))

    biases = []
    for kind, dz, to_in, to_out in ((UP, -2, bi_up, bo_up), (DOWN, 2, bi_down, bo_down)):
        to = device(0, core, x, dz)
        biases.append(remote(b_in, to_in, bias_send.at[0, kind], bias_recv.at[0, kind], to))
        biases.append(remote(b_out, to_out, bias_send.at[1, kind], bias_recv.at[1, kind], to))
    for a, k in units[:WINDOW]:
        for kind in (UP, DOWN):
            near_copy(a, k, kind).start()
    route_copies = [
        remote(routes_t, routes_around.at[side], around_send.at[1 + side], routes_recv.at[side], device(0, core, x, dz))
        for side, dz in ((0, 1), (1, -1))
    ]
    for copy in biases + route_copies:
        copy.start()

    pltpu.make_async_copy(w_in.at[0], wbi.at[0], own_sem.at[0]).start()
    pltpu.make_async_copy(w_out.at[0], wbo.at[0], own_sem.at[1]).start()

    at_row = lax.broadcasted_iota(jnp.int32, (table.shape[1], width), 0) == bucket[0]
    for k in range(3):
        for first, source in ((0, table), (3, rate)):
            mods[pl.ds(first + k, 1)] = jnp.sum(
                jnp.where(at_row, source[k].astype(F32), 0.0), axis=0, keepdims=True)
    offset, offset_tan = mods[pl.ds(0, 1)], mods[pl.ds(3, 1)]
    scale, scale_tan = 1.0 + mods[pl.ds(1, 1)], mods[pl.ds(4, 1)]

    @pl.loop(0, rows // 16)
    def _(i):
        at = pl.ds(pl.multiple_of(i * 16, 16), 16)
        values = tok[at].astype(F32)
        deltas = tan[at].astype(F32)
        center = values - jnp.mean(values, axis=-1, keepdims=True)
        spread = jnp.mean(center * center, axis=-1, keepdims=True)
        inverse = lax.rsqrt(spread + norm_eps)
        normed = center * inverse
        normed_tan = (
            deltas
            - jnp.mean(deltas, axis=-1, keepdims=True)
            - normed * jnp.mean(normed * deltas, axis=-1, keepdims=True)
        ) * inverse
        modded[at] = (normed * scale + offset).astype(BF16)
        modded_tan[at] = (normed_tan * scale + normed * scale_tan + offset_tan).astype(BF16)

    def expert_of(block, batch):
        if batch == 0:
            to_x, move = block % X, block // X - 3 * (block // (2 * X))
        elif batch == 3:
            to_x, move = block, 4
        else:
            to_x, move = block // 2, (batch + 1) * (1 - 2 * (block % 2))
        return to_x * Z + (z + move + Z) % Z

    def out_legs(batch, parts):
        first = FIRST[batch]
        for dx in range(X):
            to_x = (x + dx) % X
            if batch == 0:
                for k in range(3):
                    if k in parts:
                        yield first + k * X + to_x, first + k * X + x, device(0, core, to_x, 0), dx == 0
            elif batch == 3:
                side = dx % 2
                yield first + to_x, first + x // 2 * 2 + core, device(0, side, to_x, 1 - 2 * side), False
            else:
                for c in range(2):
                    side = (core + c) % 2
                    yield (first + to_x * 2 + side, first + x * 2 + core, device(0, side, to_x, 0),
                           (dx, c) == (0, 0))

    def home_legs(batch):
        first = FIRST[batch]
        sign = 1 - 2 * core
        if batch == 3:
            for h in range(2):
                to_x = 2 * h + (x + core) % 2
                for c in range(2):
                    yield first + 2 * h + c, first + x, device(0, c, to_x, -2 * sign), False
            return
        for dx in range(X):
            to_x = (x + dx) % X
            if batch == 0:
                for k, dz in enumerate((0, 1, -1)):
                    yield first + k * X + to_x, first + k * X + x, device(0, core, to_x, -dz), (dx, k) == (0, 0)
            else:
                for c in range(2):
                    side = (core + c) % 2
                    yield (first + to_x * 2 + side, first + x * 2 + core,
                           device(0, side, to_x, -(batch - 1) * sign), (batch, dx, c) == (1, 0, 0))

    def send_out(batch, parts=()):
        for here, there, to, own in out_legs(batch, parts):
            if own:
                pltpu.make_async_copy(tx.at[here], rx.at[there], recv_sem.at[batch]).start()
            else:
                remote(tx.at[here], rx.at[there], send_sem.at[0], recv_sem.at[batch], to).start()

    square = (rows, rows)
    down, across = lax.broadcasted_iota(jnp.int32, square, 0), lax.broadcasted_iota(jnp.int32, square, 1)
    early = (down < across).astype(F32).astype(BF16)
    late = (across < down).astype(F32).astype(BF16)
    one_t, two_t = routes_t[0:1], routes_t[1:2]

    def pack(count, move, to_x_of, slot_of, who):
        if who == 0:
            main, tan_rows, first, second = modded, modded_tan, one_t, two_t
        else:
            main, tan_rows = around.at[who - 1, 0], around.at[who - 1, 1]
            first, second = routes_around[who - 1, 0:1], routes_around[who - 1, 1:2]
        line = lax.broadcasted_iota(jnp.int32, (count * cap, rows), 0)
        base = (0, -1, 1)[who]
        expert = to_x_of(line // cap) * Z + (z + base + move(line // cap) + Z) % Z
        named = (first == expert) | (second == expert)
        rank = jnp.dot(named.astype(F32).astype(BF16), early, preferred_element_type=F32)
        pick = (named & (rank == (line % cap).astype(F32))).astype(F32).astype(BF16)

        @pl.loop(0, width // 512)
        def _(n):
            cols = pl.ds(pl.multiple_of(n * 512, 512), 512)
            for source, at in ((main, 0), (tan_rows, cap)):
                packed = jnp.dot(pick, source[:, cols], preferred_element_type=F32).astype(BF16)
                packed = packed.reshape(count, cap, 512)
                for start, size, slot in slot_of:
                    tx[pl.ds(slot, size), pl.ds(at, cap), cols] = packed[start:start + size]

    around_copies = []
    for side, dz in ((0, 1), (1, -1)):
        to = device(0, core, x, dz)
        for j, source in enumerate((modded, modded_tan)):
            around_copies.append(
                remote(source, around.at[side, j], around_send.at[0], around_recv.at[side], to))
    for copy in around_copies:
        copy.start()

    pack(4, lambda b: 0 * b, lambda b: b, [(0, 4, 0)], 0)
    send_out(0, (0,))
    pack(8, lambda b: 2 - 4 * (b % 2), lambda b: b // 2, [(0, 8, FIRST[1])], 0)
    send_out(1)

    def pack_around():
        for copy in route_copies:
            copy.wait()
        for side in range(2):
            wait_bytes(around.at[side], around_recv.at[side])
            up = 1 - 2 * side
            odd = (x + side) % 2
            pack(
                10, lambda b: up * jnp.where(b < 4, 1, jnp.where(b < 8, 3, 4)),
                lambda b: jnp.where(b < 8, b % X, 2 * (b - 8) + odd),
                [(0, 4, 4 + 4 * side)] + [(4 + j, 1, FIRST[2] + 2 * j + side) for j in range(4)]
                + [(8 + j, 1, FIRST[3] + 2 * j + odd) for j in range(2)], 1 + side)
        send_out(0, (1, 2))
        send_out(3)
        send_out(2)

    turn = (((1,), (1,)), ((), ()))
    logits = lax.dot_general(modded[...], router[...], turn, preferred_element_type=F32)
    logit_tan = lax.dot_general(modded_tan[...], router[...], turn, preferred_element_type=F32)
    one = jnp.sum(jnp.where(down == across, one_t, 0).astype(F32), axis=1, keepdims=True).astype(jnp.int32)
    second = jnp.sum(jnp.where(down == across, two_t, 0).astype(F32), axis=1, keepdims=True).astype(jnp.int32)
    lane = lax.broadcasted_iota(jnp.int32, logits.shape, 1)

    def gap(values):
        return jnp.sum(jnp.where(lane == one, values, 0.0), axis=1, keepdims=True) - jnp.sum(
            jnp.where(lane == second, values, 0.0), axis=1, keepdims=True)

    weight = 1.0 / (1.0 + jnp.exp(-gap(logits)))
    weight_tan = weight * (1.0 - weight) * gap(logit_tan)
    for batch, size in enumerate(SIZES):
        spot = lax.broadcasted_iota(jnp.int32, (rows, size * 2 * cap), 1)
        cols = pl.ds(FIRST[batch] * 2 * cap, size * 2 * cap)
        expert = expert_of(spot // (2 * cap), batch)
        is_one, is_two = one == expert, second == expert
        named = is_one | is_two
        rank = jnp.dot(late, named.astype(F32).astype(BF16), preferred_element_type=F32)
        chosen = named & (rank == (spot % cap).astype(F32))
        is_main = (spot % (2 * cap)) < cap
        share = jnp.where(is_one, weight, 1.0 - weight)
        share_tan = jnp.where(is_one, weight_tan, -weight_tan)
        for first, value in (
            (0, jnp.where(chosen & is_main, share, 0.0)),
            (rows, jnp.where(chosen, jnp.where(is_main, share_tan, share), 0.0)),
        ):
            high = value.astype(BF16)
            mix_hi[pl.ds(first, rows), cols] = high
            mix_lo[pl.ds(first, rows), cols] = (value - high.astype(F32)).astype(BF16)

    def spread_weights(a, k, kind):
        src = near[a].at[kind, pl.ds(k * step[a], step[a])]
        dst = held[a].at[1, pl.ds(dp * part[a] + k * step[a], step[a])]
        unit = a * CHUNKS + k
        send, rest = spread_send.at[kind, a], rest_sem.at[a]

        @pl.when(core == kind)
        def _():
            pltpu.make_async_copy(src, dst, rest).start()

        @pl.when(core != kind)
        def _():
            remote(src, dst, send, rest, device(0, kind, x, 0)).start()

        @pl.when(core == 0)
        def _():
            remote(src, dst, send, first_sem.at[unit, 0], device(1, kind, x, 0)).start()
            remote(src, dst, send, rest, device(-1, kind, x, 0)).start()

        @pl.when(core == 1)
        def _():
            remote(src, dst, send, rest, device(1, kind, x, 0)).start()
            remote(src, dst, send, first_sem.at[unit, 1], device(-1, kind, x, 0)).start()

    def pass_weights(a, k):
        for side, dy in ((0, 1), (1, -1)):
            piece = ((y - dy + Y) % Y) * 2 + side
            ref = held[a].at[1, pl.ds(piece * part[a] + k * step[a], step[a])]
            wait_bytes(ref, first_sem.at[a * CHUNKS + k, side])
            remote(ref, ref, pass_send.at[a], rest_sem.at[a], device(dy, core, x, 0)).start()

    def work(batch):
        place, size = min(batch, 1), SIZES[batch]
        span = size * 2 * cap
        blocks = pl.ds(FIRST[batch], size)
        wait_bytes(rx.at[blocks], recv_sem.at[batch])

        @pl.loop(0, hidden_width // 256)
        def _(n):
            cols = pl.ds(pl.multiple_of(n * 256, 256), 256)
            both = jnp.dot(
                rx[blocks].reshape(span, width), wbi[place, :, cols], preferred_element_type=F32
            ).reshape(size, 2 * cap, 256)
            hidden = both[:, :cap] + bias_in[pl.ds(place, 1), cols].reshape(1, 1, 256)
            hidden_tan = both[:, cap:]
            tanh_val = jnp.tanh(gelu_scale * (hidden + cubic_coef * hidden * hidden * hidden))
            hid[pl.ds(0, size), pl.ds(0, cap), cols] = (0.5 * hidden * (1.0 + tanh_val)).astype(BF16)
            slope = 0.5 * (1.0 + tanh_val) + 0.5 * hidden * (1.0 - tanh_val * tanh_val) * gelu_scale * (
                1.0 + 3.0 * cubic_coef * hidden * hidden
            )
            hid[pl.ds(0, size), pl.ds(cap, cap), cols] = (slope * hidden_tan).astype(BF16)

        @pl.loop(0, width // 512)
        def _(n):
            cols = pl.ds(pl.multiple_of(n * 512, 512), 512)
            both = jnp.dot(
                hid[pl.ds(0, size)].reshape(span, hidden_width), wbo[place, :, cols], preferred_element_type=F32
            ).reshape(size, 2 * cap, 512)
            rx[blocks, pl.ds(0, cap), cols] = (
                both[:, :cap] + bias_out[pl.ds(place, 1), cols].reshape(1, 1, 512)).astype(BF16)
            rx[blocks, pl.ds(cap, cap), cols] = both[:, cap:].astype(BF16)

        for here, there, to, own in home_legs(batch):
            if own:
                pltpu.make_async_copy(rx.at[here], back.at[there], ret_recv.at[batch]).start()
            else:
                remote(rx.at[here], back.at[there], ret_send.at[0], ret_recv.at[batch], to).start()

    for copy in biases:
        copy.wait()
    for bias, own, up, low in ((bias_in, b_in, bi_up, bi_down), (bias_out, b_out, bo_up, bo_down)):
        bias[pl.ds(0, 1)] = own[...]
        bias[pl.ds(1, 1)] = jnp.where(core == 0, up[...], low[...])

    def own_work():
        wait_bytes(wbi.at[0], own_sem.at[0])
        wait_bytes(wbo.at[0], own_sem.at[1])
        work(0)

    for u, (a, k) in enumerate(units):
        for kind in (UP, DOWN):
            near_copy(a, k, kind).wait_recv()
        if u + WINDOW < len(units):
            for kind in (UP, DOWN):
                near_copy(*units[u + WINDOW], kind).start()
        for kind in (UP, DOWN):
            spread_weights(a, k, kind)
        if u == RELAY_AT:
            pack_around()
        if u > 0:
            pass_weights(*units[u - 1])
        if u == EARLY:
            own_work()
    pass_weights(*units[-1])
    if EARLY >= len(units):
        own_work()
    for a in range(2):
        wait_bytes(held[a].at[1, pl.ds(0, 6 * part[a])], rest_sem.at[a])
    for batch in WORK_ORDER:
        work(batch)

    for order, batch in enumerate((0,) + WORK_ORDER):
        blocks = pl.ds(FIRST[batch], SIZES[batch])
        wait_bytes(back.at[blocks], ret_recv.at[batch])
        span = SIZES[batch] * 2 * cap
        spots = pl.ds(FIRST[batch] * 2 * cap, span)

        @pl.loop(0, width // 512)
        def _(n, order=order, blocks=blocks, span=span, spots=spots):
            cols = pl.ds(pl.multiple_of(n * 512, 512), 512)
            parts = back[blocks, :, cols].reshape(span, 512)
            mixed = jnp.dot(mix_hi[:, spots], parts, preferred_element_type=F32) + jnp.dot(
                mix_lo[:, spots], parts, preferred_element_type=F32)
            if order > 0:
                mixed = mixed + acc[:, cols]
            if order < len(WORK_ORDER):
                acc[:, cols] = mixed
            else:
                gate, gate_tan = mods[pl.ds(2, 1), cols], mods[pl.ds(5, 1), cols]
                mixture, mixture_tan = mixed[:rows], mixed[rows:]
                out[:, cols] = (tok[:, cols].astype(F32) + gate * mixture).astype(BF16)
                out_tan[:, cols] = (
                    tan[:, cols].astype(F32) + gate_tan * mixture + gate * mixture_tan).astype(BF16)

    wait_bytes(tx.at[pl.ds(0, SLOTS - 5)], send_sem.at[0])
    wait_bytes(around, around_send.at[0])
    wait_bytes(rx.at[pl.ds(0, SLOTS - 2)], ret_send.at[0])
    for a in range(2):
        wait_bytes(held[a].at[0, pl.ds(0, 2 * part[a])], near_send.at[a])
        for kind in (UP, DOWN):
            @pl.when(core == kind)
            def _(a=a, kind=kind):
                wait_bytes(held[a].at[0, pl.ds(0, 2 * part[a])], spread_send.at[kind, a])

            @pl.when(core != kind)
            def _(a=a, kind=kind):
                wait_bytes(held[a].at[0, pl.ds(0, 3 * part[a])], spread_send.at[kind, a])

        wait_bytes(held[a].at[0, pl.ds(0, 2 * part[a])], pass_send.at[a])


def local(tokens, tangent, bucket, mod_table, mod_rate, router, routes, w_in, b_in, w_out, b_out):
    rows, width = tokens.shape
    hidden_width = w_in.shape[2]
    cap = 4 * rows // router.shape[1]
    parts = lax.axis_size("dp")
    vmem = pl.BlockSpec(memory_space=pltpu.VMEM)
    smem = pl.BlockSpec(memory_space=pltpu.SMEM)
    hbm = pl.BlockSpec(memory_space=pl.ANY)
    shape = jax.ShapeDtypeStruct((rows, width), BF16)
    dma = pltpu.SemaphoreType.DMA
    units = 2 * CHUNKS
    blocks = pltpu.VMEM((SLOTS, 2 * cap, width), BF16)
    mix = pltpu.VMEM((2 * rows, SLOTS * 2 * cap), BF16)
    return tuple(pl.pallas_call(
        kernel,
        out_shape=(shape, shape),
        in_specs=[vmem, vmem, smem, vmem, vmem, vmem, vmem, hbm, vmem, hbm, vmem],
        out_specs=(vmem, vmem),
        scratch_shapes=[
            pltpu.VMEM((rows, width), BF16),
            pltpu.VMEM((rows, width), BF16),
            pltpu.VMEM((2, 2, rows, width), BF16),
            pltpu.VMEM((2, 2, rows), jnp.int32),
            blocks, blocks, blocks,
            pltpu.VMEM((2 * rows, width), F32),
            mix, mix,
            pltpu.VMEM((max(SIZES), 2 * cap, hidden_width), BF16),
            pltpu.VMEM((8, width), F32),
            pltpu.VMEM((2, width, hidden_width), BF16),
            pltpu.VMEM((2, hidden_width, width), BF16),
            pltpu.VMEM((2, width // parts, hidden_width), BF16),
            pltpu.VMEM((2, hidden_width // parts, width), BF16),
            pltpu.VMEM((2, hidden_width), F32),
            pltpu.VMEM((2, width), F32),
            *[pltpu.VMEM((1, hidden_width), F32)] * 2,
            *[pltpu.VMEM((1, width), F32)] * 2,
            dma((1,)), dma((len(SIZES),)), dma((1,)), dma((len(SIZES),)), dma((2,)),
            dma((2,)), dma((2, units)),
            dma((3,)), dma((2,)), dma((2,)),
            dma((2, 2)), dma((2,)), dma((units, 2)), dma((2,)), dma((2, 2)), dma((2, 2)),
        ],
        compiler_params=pltpu.CompilerParams(
            collective_id=0, has_side_effects=True, vmem_limit_bytes=60 << 20),
    )(tokens, tangent, bucket, mod_table.transpose(1, 0, 2), mod_rate.transpose(1, 0, 2), router.T, routes.T,
      w_in, b_in, w_out, b_out))


def solution(mesh):
    in_specs = (
        P(("dp", "seq"), None),
        P(("dp", "seq"), None),
        P("dp"),
        P(),
        P(),
        P(),
        P(("dp", "seq"), None),
        P("seq", None, None),
        P("seq", None),
        P("seq", None, None),
        P("seq", None),
    )
    out_specs = (P(("dp", "seq"), None), P(("dp", "seq"), None))
    return jax.shard_map(local, mesh=mesh, in_specs=in_specs, out_specs=out_specs, check_vma=False)
```
